128 devices in a mesh: dp: 16 (over y, z_lo, core), fsdp: 8 (over z_hi, x).
Axes of the slice: x: 4, y: 4, z: 4 (z_hi: 2, z_lo: 2; z = z_hi * 2 + z_lo), core: 2. Of those that a mesh axis runs over, the one named last changes fastest.
Arguments:
- layer_input: bfloat16 [16384, 8192], P(('dp', 'fsdp')), may hold values from -24 to 24
- queries: bfloat16 [16384, 8192], P(('dp', 'fsdp')), may hold values from -48 to 48
- key_rows: bfloat16 [16384, 1024], P(('dp', 'fsdp')), may hold values from -15 to 15
- grad_out: bfloat16 [16384, 8192], P(('dp', 'fsdp')), may hold values from -6 to 6
- w_value: bfloat16 [8192, 1024], P('fsdp'), may hold values from -0.0625 to 0.0625
- destination: int32 [16384], P(('dp', 'fsdp')), may hold values from 0 to 2047, as said below
- seg_start: int32 [16384], P(('dp', 'fsdp')), may hold values from 0 to 127, as said below
Outputs:
- grad_queries: bfloat16 [16384, 8192], P(('dp', 'fsdp'))
- grad_keys: bfloat16 [16384, 1024], P(('dp', 'fsdp'))
- grad_input: bfloat16 [16384, 8192], P(('dp', 'fsdp'))
- grad_weight: float32 [8192, 1024], P(('dp', 'fsdp'))
The draws below stay inside these ranges and needn't reach their ends.
Inputs may be any that keep to these rules, and one draw needn't show every extreme that they name: `destination`: within each fsdp index the 2048 tokens map one to one onto the packed rows of the same fsdp index. The tokens of one device go to one dp index in numbers between 6 and 10; 10 is reached by every device. seg_start[r] <= r for the row r of a device, all rows from seg_start[r] to r share it, and row 0 of every device begins a rollout.
All inputs are finite; a program needn't handle non-finite values.
Results may differ from the reference program's by a relative error of at most 0.012.
Values may be sent and summed in bfloat16 or wider, within the bound.
A program may use at most 256 MiB of HBM per device.

```python
import jax
import jax.numpy as jnp
from jax import lax

D = 8192
HEADS = 64
KV_HEADS = 8
HD = 128
TOK_DEV = 128
QW = 8192
KVW = 1024
TOKENS = 16384
N_DP = 16
N_FSDP = 8


def packing_group(group_key):
    even_share = TOK_DEV // N_DP
    swing = even_share // 4
    key_order, key_rows, key_ties, key_begin, key_single = jax.random.split(group_key, 5)
    rank_index = jnp.arange(N_DP, dtype=jnp.int32)
    item_index = jnp.arange(TOK_DEV, dtype=jnp.int32)
    rank_order = jax.random.permutation(key_order, N_DP)
    next_order = jnp.roll(rank_order, -1)
    counts = even_share + swing * (rank_order[:, None] == rank_index[None, :]).astype(jnp.int32) - swing * (next_order[:, None] == rank_index[None, :]).astype(jnp.int32)
    running = jnp.cumsum(counts, axis=0)
    owners = jnp.sum((running[:, :, None] <= item_index[None, None, :]).astype(jnp.int32), axis=0)
    row_orders = jax.vmap(lambda row_key: jax.random.permutation(row_key, TOK_DEV))(jax.random.split(key_rows, N_DP))
    slot_value = rank_index[:, None] * TOK_DEV + row_orders.astype(jnp.int32)
    tie_break = jax.random.permutation(key_ties, N_DP * TOK_DEV).astype(jnp.int32)
    sort_key = owners.reshape(-1) * (N_DP * TOK_DEV) + tie_break
    source_order = jnp.argsort(sort_key, stable=True)
    packed_row = slot_value.reshape(-1)[source_order].reshape(N_DP, TOK_DEV)
    begins = jax.random.randint(key_begin, (N_DP, TOK_DEV), 0, 32) == 0
    single_rank = jax.random.randint(key_single, (), 0, N_DP)
    last_rank = (single_rank + 1) % N_DP
    begins = jnp.where(rank_index[:, None] == single_rank, item_index[None, :] == 0, begins)
    begins = begins | (rank_index[:, None] == last_rank) & (item_index[None, :] == TOK_DEV - 1)
    begins = begins | (item_index[None, :] == 0)
    segment_begin = lax.cummax(jnp.where(begins, item_index[None, :], 0), axis=1)
    return (packed_row.astype(jnp.int32), segment_begin.astype(jnp.int32))


def packing(key):
    group_keys = jax.random.split(jax.random.fold_in(key, 977), N_FSDP)
    packed_row, segment_begin = jax.vmap(packing_group)(group_keys)
    return (jnp.transpose(packed_row, (1, 0, 2)).reshape(-1), jnp.transpose(segment_begin, (1, 0, 2)).reshape(-1))


def shared_keys(key):
    base_draw = jax.random.normal(jax.random.fold_in(key, 101), (TOKENS, KV_HEADS, HD), jnp.float32)
    return jnp.clip(base_draw, -5.0, 5.0)


def draw_destination(key, part):
    packed_row, segment_begin = packing(key)
    return packed_row


def draw_seg_start(key, part):
    packed_row, segment_begin = packing(key)
    return segment_begin


def draw_key_rows(key, part):
    shared = shared_keys(key)
    return shared.reshape(TOKENS, KV_HEADS * HD).astype(jnp.bfloat16)


def draw_queries(key, part):
    key = jax.random.fold_in(key, 13)
    key_fresh = jax.random.fold_in(key, 0)
    group_size = HEADS // KV_HEADS
    fresh = jnp.clip(jax.random.normal(key_fresh, (TOKENS, KV_HEADS, group_size, HD), jnp.float32), -6.0, 6.0)
    return fresh.reshape(TOKENS, HEADS * HD).astype(jnp.bfloat16)


def with_spikes(values, stream_key, source, target, blocks, factor):
    owner, partner = [(jnp.arange(values.shape[axis_at]) // (values.shape[axis_at] // blocks)).reshape([-1 if axis == axis_at else 1 for axis in range(values.ndim)]) for axis_at in (source, target)]
    chosen = jax.random.permutation(stream_key, blocks)[partner]
    strong = (owner == chosen) | (owner == (partner + blocks // 2) % blocks)
    return jnp.where(strong, factor * values, values)


def level_of(own_key, extent, pieces, smallest, largest):
    def one(position, parts):
        heights = jax.random.uniform(jax.random.fold_in(jax.random.fold_in(own_key, 6), position), (parts,), jnp.float32, smallest / len(pieces), largest / len(pieces))
        return jnp.repeat(jnp.exp(heights), extent[position] // parts).reshape((-1,) + (1,) * (len(extent) - position - 1))

    level = one(*pieces[0])
    for cut in pieces[1:]:
        level = level * one(*cut)
    return level


def centred(own_key, shape, deviation, bound, cuts=(), held_as=jnp.bfloat16):
    values = deviation * jax.random.normal(own_key, shape, jnp.float32)
    if cuts:
        values = values * level_of(own_key, shape, cuts, -0.22, 0.18)
    return jnp.clip(values, -bound, bound).astype(held_as)


def gaussian_with(stream_key, shape, deviation, bound, shards, heavy, kind=jnp.bfloat16):
    array = deviation * jax.random.normal(stream_key, shape, jnp.float32)
    if shards:
        array = array * level_of(stream_key, shape, shards, -0.22, 0.18)
    return jnp.clip(with_spikes(array, jax.random.fold_in(stream_key, 3), *heavy), -bound, bound).astype(kind)


def setup_inputs(seed: int = 0) -> dict:
    streams_of = jax.random.split(jax.random.key(seed), 8)
    layer_input = gaussian_with(streams_of[0], (TOKENS, D), 1.0, 24.0, ((0, 128),), (0, 1, 128, 5.5))
    queries = draw_queries(jax.random.fold_in(streams_of[7], 71), 0)
    key_rows = draw_key_rows(jax.random.fold_in(streams_of[7], 71), 0)
    grad_out = centred(streams_of[3], (TOKENS, QW), 1.0, 6.0, ((0, 128),))
    w_value = centred(streams_of[4], (D, KVW), D ** -0.5, 0.0625, ((0, 8),))
    destination = draw_destination(jax.random.fold_in(streams_of[7], 71), 0)
    seg_start = draw_seg_start(jax.random.fold_in(streams_of[7], 71), 0)
    return dict(layer_input=layer_input, queries=queries, key_rows=key_rows, grad_out=grad_out, w_value=w_value, destination=destination, seg_start=seg_start)


def attend(queries, key_rows, value_rows, grad_rows, starts):
    tokens_here = queries.shape[0]
    key_heads = key_rows.shape[1] // HD
    group_size = queries.shape[1] // key_rows.shape[1]
    query_split = queries.astype(jnp.float32).reshape(tokens_here, key_heads, group_size, HD)
    grad_split = grad_rows.astype(jnp.float32).reshape(tokens_here, key_heads, group_size, HD)
    key_split = key_rows.astype(jnp.float32).reshape(tokens_here, key_heads, HD)
    value_split = value_rows.astype(jnp.float32).reshape(tokens_here, key_heads, HD)
    inverse_root = 1.0 / (HD ** 0.5)
    positions = jnp.arange(tokens_here, dtype=jnp.int32)
    allowed = (positions[None, :] <= positions[:, None]) & (positions[None, :] >= starts[:, None])
    scores = jnp.einsum('ikgd,jkd->kgij', query_split, key_split) * inverse_root
    scores = jnp.where(allowed[None, None], scores, -1e30)
    row_peak = jnp.max(scores, axis=-1, keepdims=True)
    exponent = jnp.where(allowed[None, None], jnp.exp(scores - row_peak), 0.0)
    softmax_rows = exponent / jnp.sum(exponent, axis=-1, keepdims=True)
    softmax_low = softmax_rows.astype(jnp.bfloat16).astype(jnp.float32)
    outputs = jnp.einsum('kgij,jkd->ikgd', softmax_low, value_split)
    grad_probs = jnp.einsum('ikgd,jkd->kgij', grad_split, value_split)
    row_dots = jnp.einsum('ikgd,ikgd->kgi', grad_split, outputs)
    grad_scores = (softmax_rows * (grad_probs - row_dots[..., None])).astype(jnp.bfloat16).astype(jnp.float32)
    grad_query = (jnp.einsum('kgij,jkd->ikgd', grad_scores, key_split) * inverse_root).astype(jnp.bfloat16)
    grad_key = (jnp.einsum('kgij,ikgd->jkd', grad_scores, query_split) * inverse_root).astype(jnp.bfloat16)
    grad_value = jnp.einsum('kgij,ikgd->jkd', softmax_low, grad_split).astype(jnp.bfloat16)
    return (grad_query.reshape(tokens_here, -1), grad_key.reshape(tokens_here, -1),
            grad_value.reshape(tokens_here, -1))


def reference(layer_input, queries, key_rows, grad_out, w_value, destination, seg_start):
    values = jnp.dot(layer_input, w_value, preferred_element_type=jnp.float32).astype(jnp.bfloat16)
    token_index = jnp.arange(TOKENS, dtype=jnp.int32)
    fsdp_index = (token_index // TOK_DEV) % N_FSDP
    packed = (((destination // TOK_DEV) * N_FSDP + fsdp_index) * TOK_DEV + destination % TOK_DEV).astype(jnp.int32)
    blocks = N_DP * N_FSDP

    def place(data):
        return jnp.zeros_like(data).at[packed].set(data).reshape(blocks, TOK_DEV, data.shape[1])

    stacked = (place(queries), place(key_rows), place(values), place(grad_out),
               seg_start.reshape(blocks, TOK_DEV))

    def per_block(items):
        return attend(items[0], items[1], items[2], items[3], items[4])

    packed_dq, packed_dk, packed_dv = lax.map(per_block, stacked)
    grad_queries = packed_dq.reshape(TOKENS, -1)[packed]
    grad_keys = packed_dk.reshape(TOKENS, -1)[packed]
    grad_values = packed_dv.reshape(TOKENS, -1)[packed]
    grad_input = jnp.dot(grad_values, w_value.T, preferred_element_type=jnp.float32).astype(jnp.bfloat16)
    grad_weight = jnp.dot(layer_input.T, grad_values, preferred_element_type=jnp.float32)
    return grad_queries, grad_keys, grad_input, grad_weight
```

```python
import functools

import jax
import jax.numpy as jnp
from jax import lax
from jax.experimental import pallas as pl
from jax.experimental.pallas import tpu as pltpu
from jax.sharding import PartitionSpec as P

MESH = pl.DeviceIdType.MESH
F32 = jnp.float32
BF16 = jnp.bfloat16
HD = 128
ROWS = 128
RANKS = 16
SLOTS = 16
KVH = 8
GROUP = 8
KVW = KVH * HD
HALF = 512
INV_ROOT = 1.0 / HD**0.5
LOG2E = 1.4426950408889634
CHIP_STEPS = ((1, 0), (3, 0), (0, 1), (1, 1), (3, 1), (2, 0), (2, 1))
LINE_STEPS = ((1, 0), (3, 0), (1, 1), (3, 1), (2, 0), (2, 1), (0, 1))


def dot(a, b):
    return jnp.dot(a, b, preferred_element_type=F32)


def dot_nt(a, b):
    return lax.dot_general(a, b, (((1,), (1,)), ((), ())), preferred_element_type=F32)


def dot_tn(a, b):
    return lax.dot_general(a, b, (((0,), (0,)), ((), ())), preferred_element_type=F32)


def device(y, zl, c, zh, x):
    return (y * 4 + zl * 2 + c, zh * 4 + x)


def kernel(
    li_ref, q_ref, k_ref, go_ref, w_ref, dest_ref, seg_ref,
    gq_ref, gk_ref, gi_ref, gw_ref,
    ka, va, qs, gos, xs, probs, li, wm, vp, vsib, vrow, dbuf, sb1, rb1, sb2, rb2, gva, gwb, gwr,
    sel, put, posl, startl, tmp,
    loc_sem, k_sem, kf_sem, v_sem, vf_sem, li_sem, w_sem, vs_sem, vx_sem,
    s1_sem, r1_sem, s2_sem, r2_sem, gx_sem, gf_sem, gi_sem, gws_sem, gwr_sem, out_sem,
):
    d, f = lax.axis_index("dp"), lax.axis_index("fsdp")
    y, zl, c = d // 4, lax.rem(d // 2, 2), lax.rem(d, 2)
    zh, x = f // 4, lax.rem(f, 4)
    z = zh * 2 + zl
    sib = device(y, zl, 1 - c, zh, x)

    def chip_at(step, sign):
        return lax.rem(y + sign * step[0] + 4, 4), lax.rem(zl + step[1], 2)

    def chip_dev(step, sign=1):
        ty, tz = chip_at(step, sign)
        return device(ty, tz, c, zh, x)

    def chip_index(step, sign=1):
        ty, tz = chip_at(step, sign)
        return ty * 2 + tz

    def line_at(step, sign=1):
        return lax.rem(x + sign * step[0] + 4, 4), lax.rem(c + step[1], 2)

    def line_dev(step, sign=1):
        tx, tc = line_at(step, sign)
        return device(y, zl, tc, zh, tx)

    def remote(src, dst, ssem, rsem, dev):
        return pltpu.make_async_remote_copy(
            src_ref=src, dst_ref=dst, send_sem=ssem, recv_sem=rsem, device_id=dev, device_id_type=MESH
        )

    own_k = pltpu.make_async_copy(k_ref, ka.at[d, pl.ds(0, ROWS)], loc_sem.at[0])
    own_k.start()
    q_loads = []
    for g in range(KVH):
        cols = pl.ds(g * 1024, 1024)
        a = pltpu.make_async_copy(q_ref.at[:, cols], dbuf.at[0, g], loc_sem.at[1 + g])
        b = pltpu.make_async_copy(go_ref.at[:, cols], dbuf.at[1, g], loc_sem.at[9 + g])
        a.start()
        b.start()
        q_loads += [(a, b)]
    me_line = c * 4 + x
    li_own = []
    for h in range(2):
        e = pltpu.make_async_copy(
            li_ref.at[:, pl.ds(pl.multiple_of(h * 4096 + x * 1024 + c * HALF, HALF), HALF)],
            li.at[h, me_line],
            loc_sem.at[17 + h],
        )
        e.start()
        li_own += [e]
    own_rows = w_ref.at[pl.ds(pl.multiple_of(c * HALF, HALF), HALF)]
    w_own = pltpu.make_async_copy(own_rows, wm.at[zh], loc_sem.at[19])
    w_own.start()

    barrier = pltpu.get_barrier_semaphore()

    def greet(dev):
        pl.semaphore_signal(barrier, inc=1, device_id=dev, device_id_type=MESH)

    w_dev = device(y, 1 - zl, c, 1 - zh, x)
    x_src = lax.rem(y, 2) * 2 + zl
    in_own_line = x == x_src
    for step in CHIP_STEPS:
        greet(chip_dev(step, -1))
    for step in LINE_STEPS:
        greet(line_dev(step, -1))
    greet(w_dev)
    for i in range(16):
        sy, sz = i // 4, i % 4

        @pl.when(jnp.logical_not(in_own_line & (y == sy) & (z == sz)))
        def _():
            greet(device(sy, sz % 2, c, sz // 2, x_src))

    pl.semaphore_wait(barrier, 7 + 7 + 1 + 16 - in_own_line.astype(jnp.int32))

    dest = jnp.broadcast_to(dest_ref[...], (SLOTS, ROWS))
    block = (dest >> 7).astype(F32)
    label = (dest & 127).astype(F32) + 1.0
    seg = jnp.broadcast_to(seg_ref[...], (SLOTS, ROWS)).astype(F32)
    ka[d, ROWS:, :] = jnp.concatenate(
        [block, label, seg] + [jnp.zeros((SLOTS, ROWS), F32)] * 5, axis=1
    ).astype(BF16)
    own_k.wait()

    def gather_start(buf, sems, fsems):
        copies = []
        for o, step in enumerate(CHIP_STEPS):
            r = remote(buf.at[d], buf.at[d], sems.at[0, o], sems.at[1, o], chip_dev(step))
            r.start()
            copies += [r]
        fwd = [remote(buf.at[d], buf.at[d], fsems.at[0, 7], fsems.at[1, 7], sib)]
        fwd[0].start()
        return copies, fwd

    k_copies, k_fwd = gather_start(ka, k_sem, kf_sem)
    li_copies = []
    for o, step in enumerate(LINE_STEPS):
        tx, tc = line_at(step)
        for h in range(2):
            r = remote(
                li_ref.at[:, pl.ds(pl.multiple_of(h * 4096 + tx * 1024 + tc * HALF, HALF), HALF)],
                li.at[h, me_line],
                li_sem.at[0, o * 2 + h],
                li_sem.at[1, o * 2 + h],
                line_dev(step),
            )
            r.start()
            li_copies += [r]
    w_copy = remote(own_rows, wm.at[zh], w_sem.at[0], w_sem.at[1], w_dev)
    w_copy.start()

    rows16 = lax.broadcasted_iota(jnp.int32, (SLOTS, ROWS), 0).astype(F32)
    tri = (
        lax.broadcasted_iota(jnp.int32, (ROWS, ROWS), 0)
        < lax.broadcasted_iota(jnp.int32, (ROWS, ROWS), 1)
    ).astype(F32).astype(BF16)
    ones = jnp.ones((ROWS, ROWS), BF16)
    rows256 = lax.broadcasted_iota(jnp.int32, (256, ROWS), 0).astype(F32)
    lane1 = lax.broadcasted_iota(jnp.int32, (ROWS, ROWS), 1).astype(F32) + 1.0
    lane1_256 = lax.broadcasted_iota(jnp.int32, (256, ROWS), 1).astype(F32) + 1.0
    low4 = (lax.broadcasted_iota(jnp.int32, (ROWS, ROWS), 0) & 15).astype(F32)

    def slots_of(block16):
        hot = (block16 == rows16).astype(F32)
        rank = jnp.sum(hot * dot(hot.astype(BF16), tri), axis=0, keepdims=True)
        return block16[0:1] * SLOTS + rank

    own_slot = slots_of(block)
    own_sel = (rows256 == own_slot).astype(F32).astype(BF16)

    for g in range(KVH):
        for which, dst in ((0, qs), (1, gos)):
            q_loads[g][which].wait()
            placed = dot(own_sel, dbuf[which, g]).astype(BF16)
            for h in range(GROUP):
                dst[:, g, h * SLOTS : (h + 1) * SLOTS, :] = placed[:, h * HD : (h + 1) * HD].reshape(
                    RANKS, SLOTS, HD
                )

    def take_keys(s):
        extra = ka[s, ROWS:, 0:384].astype(F32)
        block_s, label_s, seg_s = extra[:, 0:128], extra[:, 128:256], extra[:, 256:384]
        hot = (rows256 == slots_of(block_s)).astype(F32)
        hot_low = hot.astype(BF16)
        sel[s] = hot_low
        labels = dot((hot * label_s[0:1]).astype(BF16), ones)
        put[:, s] = (labels == lane1_256).astype(F32).astype(BF16).reshape(RANKS, SLOTS, ROWS)
        xs[:, s] = dot(hot_low, ka[s, 0:ROWS, :]).astype(BF16).reshape(RANKS, SLOTS, KVW)
        mine = (low4 + (s * SLOTS).astype(F32) == own_slot).astype(F32)
        columns = dot((mine * label[0:1]).astype(BF16), ones)
        at_row = (columns == lane1).astype(F32).astype(BF16)
        posl[s] = dot_nt(label.astype(BF16), mine.astype(BF16)) - 1.0
        startl[s] = dot_nt(seg_s.astype(BF16), at_row)

    def take_values(s):
        xs[:, s] = dot(sel[s], va[s]).astype(BF16).reshape(RANKS, SLOTS, KVW)

    def gather_finish(buf, sems, fsems, copies, fwd, take):
        take(d)
        fwd[0].wait_recv()
        take(y * 4 + zl * 2 + 1 - c)
        pending = None
        for o, step in enumerate(CHIP_STEPS):
            src = chip_index(step, -1) * 2 + c
            copies[o].wait_recv()
            r = remote(buf.at[src], buf.at[src], fsems.at[0, o], fsems.at[1, o], sib)
            r.start()
            fwd += [r]
            take(src)
            if pending is not None:
                pending[0].wait_recv()
                take(pending[1])
            pending = (r, chip_index(step, -1) * 2 + 1 - c)
        pending[0].wait_recv()
        take(pending[1])

    gather_finish(ka, k_sem, kf_sem, k_copies, k_fwd, take_keys)

    for e in li_own:
        e.wait()
    w_own.wait()
    for r in li_copies:
        r.wait_recv()
    w_copy.wait_recv()

    def value_term(core):
        def chunk(n, _):
            cols = pl.ds(pl.multiple_of(n * 256, 256), 256)
            part = dot(li[0, pl.ds(core * 4, 4)].reshape(HALF, HALF), wm[0, :, cols])
            part += dot(li[1, pl.ds(core * 4, 4)].reshape(HALF, HALF), wm[1, :, cols])
            vp[pl.ds(core * 4, 4), :, cols] = part.astype(BF16).reshape(4, ROWS, 256)
            return 0

        lax.fori_loop(0, 4, chunk, 0)

    value_term(1 - c)
    v_sib = remote(
        vp.at[pl.ds((1 - c) * 4, 4)], vsib, vs_sem.at[0], vs_sem.at[1], sib
    )
    v_sib.start()
    value_term(c)

    for r in k_copies + k_fwd:
        r.wait_send()

    def mask_of(t):
        j = lax.broadcasted_iota(jnp.int32, (ROWS, ROWS), 0).astype(F32)
        return (j <= posl[t][0:1]) & (j >= startl[t][0:1])

    def first_pass(t, _):
        put_t = put[t].reshape(256, ROWS)
        ka[t, 0:ROWS, :] = dot_tn(put_t, xs[t].reshape(256, KVW)).astype(BF16)
        allowed = mask_of(t)
        for g in range(KVH):
            cols = slice(g * HD, (g + 1) * HD)
            scores = dot_nt(ka[t, 0:ROWS, cols], qs[t, g]) * (INV_ROOT * LOG2E)
            scores = jnp.where(allowed, scores, -1e30)
            peak = jnp.maximum(jnp.max(scores, axis=0, keepdims=True), -1e29)
            expo = jnp.exp2(scores - peak)
            total = jnp.maximum(jnp.sum(expo, axis=0, keepdims=True), 0.5)
            low = (expo * (1.0 / total)).astype(BF16)
            probs[t, g] = low
            tmp[:, cols] = dot(low, gos[t, g]).astype(BF16)
        xs[t] = dot(put_t, tmp[...]).astype(BF16).reshape(RANKS, SLOTS, KVW)
        return 0

    lax.fori_loop(0, 8, first_pass, 0)

    v_sib.wait_recv()
    vx = []
    own_v = None
    for o, dx in enumerate((0, 1, 3, 2)):
        tx = lax.rem(x + dx, 4)
        total = vp[c * 4 + tx].astype(F32) + vsib[tx].astype(F32)
        if dx == 0:
            own_v = total
        else:
            vp[c * 4 + tx] = total.astype(BF16)
            r = remote(
                vp.at[c * 4 + tx], vrow.at[o - 1], vx_sem.at[0, o - 1], vx_sem.at[1, o - 1],
                device(y, zl, c, zh, tx),
            )
            r.start()
            vx += [r]

    lax.fori_loop(8, 16, first_pass, 0)

    vsum = own_v
    for o in range(3):
        vx[o].wait_recv()
        vsum = vsum + vrow[o].astype(F32)
    va[d] = vsum.astype(BF16)
    v_copies, v_fwd = gather_start(va, v_sem, vf_sem)

    def scatter_start(sb, rb, ssems, rsems):
        sib_copies, out_copies = [], []
        for q in range(8):
            s = q * 2 + 1 - c
            dbuf[1 - c, q] = dot_tn(sel[s], xs[:, s].reshape(256, KVW)).astype(BF16)
            r = remote(dbuf.at[1 - c, q], sb.at[q], ssems.at[0, q], ssems.at[1, q], sib)
            r.start()
            sib_copies += [r]
        for r in sib_copies:
            r.wait_recv()
        for o, step in enumerate(CHIP_STEPS + ((0, 0),)):
            q = chip_index(step)
            s = q * 2 + c
            part = dot_tn(sel[s], xs[:, s].reshape(256, KVW)) + sb[q].astype(F32)
            dbuf[c, q] = part.astype(BF16)
            if o < 7:
                r = remote(dbuf.at[c, q], rb.at[o], rsems.at[0, o], rsems.at[1, o], chip_dev(step))
                r.start()
                out_copies += [r]
        return sib_copies, out_copies

    def scatter_finish(rb, out_copies):
        total = dbuf[c, y * 2 + zl].astype(F32)
        for o in range(7):
            out_copies[o].wait_recv()
            total = total + rb[o].astype(F32)
        return total.astype(BF16)

    s1_copies, r1_copies = scatter_start(sb1, rb1, s1_sem, r1_sem)
    gva[me_line] = scatter_finish(rb1, r1_copies)

    gx = []
    gf = []
    for o, dx in enumerate((1, 3, 2)):
        r = remote(
            gva.at[me_line], gva.at[me_line], gx_sem.at[0, o], gx_sem.at[1, o],
            device(y, zl, c, zh, lax.rem(x + dx, 4)),
        )
        r.start()
        gx += [r]
    r = remote(gva.at[me_line], gva.at[me_line], gf_sem.at[0, 3], gf_sem.at[1, 3], sib)
    r.start()
    gf += [r]
    for o, dx in enumerate((1, 3, 2)):
        src = c * 4 + lax.rem(x - dx + 4, 4)
        gx[o].wait_recv()
        r = remote(gva.at[src], gva.at[src], gf_sem.at[0, o], gf_sem.at[1, o], sib)
        r.start()
        gf += [r]
    for r in vx + [v_sib]:
        r.wait_send()
    for r in gf:
        r.wait_recv()

    def input_term(j, _):
        for h in range(2):
            vp[j, :, h * HALF : (h + 1) * HALF] = dot_nt(gva[j], wm[h]).astype(BF16)
        return 0

    lax.fori_loop(0, 8, input_term, 0)
    gi_cols = [pl.ds(pl.multiple_of(h * 4096 + x * 1024 + c * HALF, HALF), HALF) for h in range(2)]
    gi_copies = []
    gi_own = []
    for h in range(2):
        e = pltpu.make_async_copy(
            vp.at[me_line, :, pl.ds(h * HALF, HALF)], gi_ref.at[:, gi_cols[h]], loc_sem.at[20 + h]
        )
        e.start()
        gi_own += [e]
    for o, step in enumerate(LINE_STEPS):
        tx, tc = line_at(step)
        for h in range(2):
            r = remote(
                vp.at[tc * 4 + tx, :, pl.ds(h * HALF, HALF)], gi_ref.at[:, gi_cols[h]],
                gi_sem.at[0, o * 2 + h], gi_sem.at[1, o * 2 + h], line_dev(step),
            )
            r.start()
            gi_copies += [r]

    def weight_term(n, _):
        h, cols = n // 4, pl.ds(pl.multiple_of(lax.rem(n, 4) * 256, 256), 256)
        part = dot_tn(li[h].reshape(1024, HALF), gva[:, :, cols].reshape(1024, 256))
        gwb[h, :, :, cols] = part.astype(BF16).reshape(8, 64, 256)
        return 0

    lax.fori_loop(0, 8, weight_term, 0)
    my_slot = y * 4 + z
    for h in range(2):
        for fb in range(8):
            to_self = in_own_line & (y // 2 == h) & (f == fb)
            dev = device(2 * h + x // 2, lax.rem(x, 2), c, fb // 4, fb % 4)

            @pl.when(to_self)
            def _():
                pltpu.make_async_copy(gwb.at[h, fb], gwr.at[my_slot], gwr_sem.at[my_slot]).start()

            @pl.when(jnp.logical_not(to_self))
            def _():
                remote(
                    gwb.at[h, fb], gwr.at[my_slot], gws_sem.at[h * 8 + fb], gwr_sem.at[my_slot], dev
                ).start()

    gather_finish(va, v_sem, vf_sem, v_copies, v_fwd, take_values)

    def second_pass(t, _):
        put_t = put[t].reshape(256, ROWS)
        tmp[...] = dot_tn(put_t, xs[t].reshape(256, KVW)).astype(BF16)
        for g in range(KVH):
            cols = slice(g * HD, (g + 1) * HD)
            grad = gos[t, g]
            grad_probs = dot_nt(tmp[:, cols], grad)
            low = probs[t, g].astype(F32)
            row_dots = jnp.sum(low * grad_probs, axis=0, keepdims=True)
            grad_scores = (low * (grad_probs - row_dots)).astype(BF16)
            tmp[:, cols] = (dot(grad_scores, qs[t, g]) * INV_ROOT).astype(BF16)
            qs[t, g] = (dot_tn(grad_scores, ka[t, 0:ROWS, cols]) * INV_ROOT).astype(BF16)
        xs[t] = dot(put_t, tmp[...]).astype(BF16).reshape(RANKS, SLOTS, KVW)
        return 0

    lax.fori_loop(0, 16, second_pass, 0)
    for r in s1_copies + r1_copies + v_copies + v_fwd:
        r.wait_send()
    s2_copies, r2_copies = scatter_start(sb2, rb2, s2_sem, r2_sem)

    q_out = []
    for g in range(KVH):
        slots = jnp.concatenate(
            [qs[:, g, h * SLOTS : (h + 1) * SLOTS, :].reshape(256, HD) for h in range(GROUP)], axis=1
        )
        va[g] = dot_tn(own_sel, slots).astype(BF16)
        e = pltpu.make_async_copy(va.at[g], gq_ref.at[:, pl.ds(g * 1024, 1024)], out_sem.at[g])
        e.start()
        q_out += [e]

    gw_total = jnp.zeros((64, KVW), F32)
    for i in range(16):
        pltpu.make_async_copy(gwr.at[i], gwr.at[i], gwr_sem.at[i]).wait()
        gw_total = gw_total + gwr[i].astype(F32)
    gw_ref[...] = gw_total
    gk_ref[...] = scatter_finish(rb2, r2_copies)

    for r in gi_copies:
        r.wait()
    for e in gi_own + q_out:
        e.wait()
    for r in li_copies + [w_copy] + s2_copies + r2_copies + gx + gf:
        r.wait_send()
    for h in range(2):
        for fb in range(8):
            to_self = in_own_line & (y // 2 == h) & (f == fb)

            @pl.when(jnp.logical_not(to_self))
            def _():
                remote(
                    gwb.at[h, fb], gwr.at[my_slot], gws_sem.at[h * 8 + fb], gwr_sem.at[my_slot],
                    device(2 * h + x // 2, lax.rem(x, 2), c, fb // 4, fb % 4),
                ).wait_send()


def shards(layer_input, queries, key_rows, grad_out, w_value, destination, seg_start):
    any_spec = pl.BlockSpec(memory_space=pl.ANY)
    vmem_spec = pl.BlockSpec(memory_space=pltpu.VMEM)
    dma = pltpu.SemaphoreType.DMA
    tokens = pltpu.VMEM
    return pl.pallas_call(
        kernel,
        out_shape=(
            jax.ShapeDtypeStruct(queries.shape, BF16),
            jax.ShapeDtypeStruct(key_rows.shape, BF16),
            jax.ShapeDtypeStruct(layer_input.shape, BF16),
            jax.ShapeDtypeStruct((64, KVW), F32),
        ),
        in_specs=[any_spec] * 5 + [vmem_spec] * 2,
        out_specs=(any_spec, vmem_spec, any_spec, vmem_spec),
        scratch_shapes=[
            tokens((RANKS, ROWS + SLOTS, KVW), BF16),
            tokens((RANKS, ROWS, KVW), BF16),
            tokens((RANKS, KVH, ROWS, HD), BF16),
            tokens((RANKS, KVH, ROWS, HD), BF16),
            tokens((RANKS, RANKS, SLOTS, KVW), BF16),
            tokens((RANKS, KVH, ROWS, ROWS), BF16),
            tokens((2, 8, ROWS, HALF), BF16),
            tokens((2, HALF, KVW), BF16),
            tokens((8, ROWS, KVW), BF16),
            tokens((4, ROWS, KVW), BF16),
            tokens((3, ROWS, KVW), BF16),
            tokens((2, 8, ROWS, KVW), BF16),
            tokens((8, ROWS, KVW), BF16),
            tokens((7, ROWS, KVW), BF16),
            tokens((8, ROWS, KVW), BF16),
            tokens((7, ROWS, KVW), BF16),
            tokens((8, ROWS, KVW), BF16),
            tokens((2, 8, 64, KVW), BF16),
            tokens((16, 64, KVW), BF16),
            tokens((RANKS, 256, ROWS), BF16),
            tokens((RANKS, RANKS, SLOTS, ROWS), BF16),
            tokens((RANKS, SLOTS, ROWS), F32),
            tokens((RANKS, SLOTS, ROWS), F32),
            tokens((ROWS, KVW), BF16),
            dma((22,)),
            dma((2, 7)),
            dma((2, 8)),
            dma((2, 7)),
            dma((2, 8)),
            dma((2, 14)),
            dma((2,)),
            dma((2,)),
            dma((2, 3)),
            dma((2, 8)),
            dma((2, 7)),
            dma((2, 8)),
            dma((2, 7)),
            dma((2, 3)),
            dma((2, 4)),
            dma((2, 14)),
            dma((16,)),
            dma((16,)),
            dma((8,)),
        ],
        name="packed_backward",
        compiler_params=pltpu.CompilerParams(
            collective_id=0, has_side_effects=True, vmem_limit_bytes=64 * 1024 * 1024
        ),
    )(
        layer_input, queries, key_rows, grad_out, w_value,
        destination.reshape(1, ROWS), seg_start.reshape(1, ROWS),
    )


def solution(mesh):
    both = P(("dp", "fsdp"), None)
    return jax.shard_map(
        shards,
        mesh=mesh,
        in_specs=(both, both, both, both, P("fsdp", None), P(("dp", "fsdp")), P(("dp", "fsdp"))),
        out_specs=(both, both, both, both),
        check_vma=False,
    )
```

```python
import functools

import jax
import jax.numpy as jnp
from jax import lax
from jax.experimental import pallas as pl
from jax.experimental.pallas import tpu as pltpu
from jax.sharding import PartitionSpec as P

MESH = pl.DeviceIdType.MESH
F32 = jnp.float32
BF16 = jnp.bfloat16
HD = 128
ROWS = 128
RANKS = 16
SLOTS = 16
KVH = 8
GROUP = 8
KVW = KVH * HD
HALF = 512
KEYS = 160
INV_ROOT = 1.0 / HD**0.5
LOG2E = 1.4426950408889634
LINE_STEPS = ((1, 0), (3, 0), (1, 1), (3, 1), (2, 0), (2, 1), (0, 1))


def dot(a, b):
    return jnp.dot(a, b, preferred_element_type=F32)


def dot_nt(a, b):
    return lax.dot_general(a, b, (((1,), (1,)), ((), ())), preferred_element_type=F32)


def dot_tn(a, b):
    return lax.dot_general(a, b, (((0,), (0,)), ((), ())), preferred_element_type=F32)


def device(y, zl, c, zh, x):
    return (y * 4 + zl * 2 + c, zh * 4 + x)


def kernel(
    li_ref, q_ref, k_ref, go_ref, w_ref, dest_ref, seg_ref,
    gq_ref, gk_ref, gi_ref, gw_ref,
    ka, va, qs, gos, xa, xb, probs, li, wm, vp, vsib, vrow, sb1, rb1, sb2, rb2, gva,
    ga, gb, ra, rbb, gwa, gwb, sel, selo, labk, labo, posl, startl,
    loc_sem, k_sem, kf_sem, v_sem, vf_sem, li_sem, w_sem, vs_sem, vx_sem,
    s1_sem, r1_sem, s2_sem, r2_sem, gx_sem, gf_sem, gi_sem, g1_sem, g2s_sem, g2r_sem, out_sem,
):
    d, f = lax.axis_index("dp"), lax.axis_index("fsdp")
    y, zl, c = d // 4, lax.rem(d // 2, 2), lax.rem(d, 2)
    zh, x = f // 4, lax.rem(f, 4)
    z = zh * 2 + zl
    sib = device(y, zl, 1 - c, zh, x)
    y_up, y_down, y_far = lax.rem(y + 1, 4), lax.rem(y + 3, 4), lax.rem(y + 2, 4)
    dev_up, dev_down = device(y_up, zl, c, zh, x), device(y_down, zl, c, zh, x)
    dev_z = device(y, 1 - zl, c, zh, x)

    def line_at(step, sign=1):
        return lax.rem(x + sign * step[0] + 4, 4), lax.rem(c + step[1], 2)

    def line_dev(step, sign=1):
        tx, tc = line_at(step, sign)
        return device(y, zl, tc, zh, tx)

    def remote(src, dst, ssem, rsem, dev):
        return pltpu.make_async_remote_copy(
            src_ref=src, dst_ref=dst, send_sem=ssem, recv_sem=rsem, device_id=dev, device_id_type=MESH
        )

    own_k = pltpu.make_async_copy(k_ref, ka.at[d, pl.ds(0, ROWS)], loc_sem.at[0])
    own_k.start()

    def load(ref, g, sem):
        e = pltpu.make_async_copy(ref.at[:, pl.ds(g * 1024, 1024)], vp.at[g], sem)
        e.start()
        return e

    q_loads = [load(q_ref, g, loc_sem.at[1 + g]) for g in range(KVH)]
    me_line = c * 4 + x
    li_own = []
    for h in range(2):
        e = pltpu.make_async_copy(
            li_ref.at[:, pl.ds(pl.multiple_of(h * 4096 + x * 1024 + c * HALF, HALF), HALF)],
            li.at[h, me_line],
            loc_sem.at[17 + h],
        )
        e.start()
        li_own += [e]
    own_rows = w_ref.at[pl.ds(pl.multiple_of(c * HALF, HALF), HALF)]
    w_own = pltpu.make_async_copy(own_rows, wm.at[zh], loc_sem.at[19])
    w_own.start()

    barrier = pltpu.get_barrier_semaphore()

    def greet(dev):
        pl.semaphore_signal(barrier, inc=1, device_id=dev, device_id_type=MESH)

    w_dev = device(y, 1 - zl, c, 1 - zh, x)
    z_devs = [device(y, lax.rem(z + i, 2), c, lax.rem(z + i, 4) // 2, x) for i in (1, 2, 3)]
    y_devs = [device(lax.rem(y + i, 4), zl, c, zh, x) for i in (1, 2, 3)]
    x_src = lax.rem(y, 2) * 2 + zl
    in_own_line = x == x_src
    for dev in [dev_up, dev_down, dev_z, w_dev] + z_devs + y_devs:
        greet(dev)
    for step in LINE_STEPS:
        greet(line_dev(step, -1))
    y_src = 2 * (y // 2) + x // 2
    for i in range(4):

        @pl.when(jnp.logical_not(in_own_line & (y == i) & (zl == lax.rem(x, 2))))
        def _():
            greet(device(i, lax.rem(x, 2), c, zh, x_src))

        @pl.when(jnp.logical_not(in_own_line & (y == y_src) & (z == i)))
        def _():
            greet(device(y_src, i % 2, c, i // 2, x_src))

    pl.semaphore_wait(barrier, 10 + 7 + 8 - 2 * in_own_line.astype(jnp.int32))

    dest = jnp.broadcast_to(dest_ref[...], (SLOTS, ROWS))
    block = (dest >> 7).astype(F32)
    label = (dest & 127).astype(F32) + 1.0
    seg = jnp.broadcast_to(seg_ref[...], (SLOTS, ROWS)).astype(F32)
    ka[d, ROWS:, :] = jnp.concatenate(
        [block, label, seg] + [jnp.zeros((SLOTS, ROWS), F32)] * 5, axis=1
    ).astype(BF16)
    own_k.wait()

    class Gather:
        def __init__(self, buf, rows, sems, fsems):
            chips = [(y, zl), (y, 1 - zl), (y_down, zl), (y_up, zl)]
            chips += [(y_down, 1 - zl), (y_up, 1 - zl), (y_far, zl), (y_far, 1 - zl)]
            self.q = [cy * 2 + cz for cy, cz in chips]
            me, zs, yd, yu, _, _, yo, _ = [q * 2 + c for q in self.q]

            def hop(i, slot, dev, first=0, count=rows):
                part = buf.at[slot, pl.ds(first, count)]
                return remote(part, part, sems.at[0, i], sems.at[1, i], dev)

            self.hops = [
                hop(0, me, dev_up), hop(1, me, dev_down), hop(2, me, dev_z),
                hop(3, zs, dev_up), hop(4, zs, dev_down),
                hop(5, yd, dev_up, 0, 64), hop(6, yu, dev_down, 64, rows - 64),
                hop(7, yo, dev_z),
            ]
            self.twin = [
                remote(buf.at[q * 2 + c], buf.at[q * 2 + c], fsems.at[0, j], fsems.at[1, j], sib)
                for j, q in enumerate(self.q)
            ]

        def start(self):
            for r in self.hops[:3] + self.twin[:1]:
                r.start()

        def second(self):
            hops, twin = self.hops, self.twin
            hops[2].wait_recv()
            for r in (hops[3], hops[4], twin[1]):
                r.start()
            hops[0].wait_recv()
            for r in (hops[5], twin[2]):
                r.start()
            hops[1].wait_recv()
            for r in (hops[6], twin[3]):
                r.start()

        def third(self):
            hops, twin = self.hops, self.twin
            hops[5].wait_recv()
            hops[6].wait_recv()
            for r in (hops[7], twin[6]):
                r.start()
            hops[3].wait_recv()
            twin[4].start()
            hops[4].wait_recv()
            twin[5].start()

        def fourth(self):
            self.hops[7].wait_recv()
            self.twin[7].start()

        def take(self, which, taker):
            for j in which:
                self.twin[j].wait_recv()
                taker(self.q[j])

        def drain(self):
            for r in self.hops + self.twin:
                r.wait_send()

    keys = Gather(ka, ROWS + SLOTS, k_sem, kf_sem)
    keys.start()
    li_copies = []
    for o, step in enumerate(LINE_STEPS):
        tx, tc = line_at(step)
        for h in range(2):
            r = remote(
                li_ref.at[:, pl.ds(pl.multiple_of(h * 4096 + tx * 1024 + tc * HALF, HALF), HALF)],
                li.at[h, me_line],
                li_sem.at[0, o * 2 + h],
                li_sem.at[1, o * 2 + h],
                line_dev(step),
            )
            r.start()
            li_copies += [r]
    w_copy = remote(own_rows, wm.at[zh], w_sem.at[0], w_sem.at[1], w_dev)
    w_copy.start()

    rows16 = lax.broadcasted_iota(jnp.int32, (SLOTS, ROWS), 0).astype(F32)
    tri = (
        lax.broadcasted_iota(jnp.int32, (ROWS, ROWS), 0)
        < lax.broadcasted_iota(jnp.int32, (ROWS, ROWS), 1)
    ).astype(F32).astype(BF16)
    ones = jnp.ones((ROWS, ROWS), BF16)
    rows256 = lax.broadcasted_iota(jnp.int32, (256, ROWS), 0).astype(F32)
    lane1 = lax.broadcasted_iota(jnp.int32, (ROWS, ROWS), 1).astype(F32) + 1.0
    low4 = (lax.broadcasted_iota(jnp.int32, (ROWS, ROWS), 0) & 15).astype(F32)

    def ranks_of(block16):
        hot = (block16 == rows16).astype(F32)
        return jnp.sum(hot * dot(hot.astype(BF16), tri), axis=0, keepdims=True)

    own_slot = block[0:1] * SLOTS + ranks_of(block)
    own_sel = (rows256 == own_slot).astype(F32).astype(BF16)

    def by_block(g, dst):
        placed = dot(own_sel, vp[g]).astype(BF16)
        for h in range(GROUP):
            dst[:, g, h * SLOTS : (h + 1) * SLOTS, :] = placed[:, h * HD : (h + 1) * HD].reshape(
                RANKS, SLOTS, HD
            )

    go_loads = []
    for g in range(KVH):
        q_loads[g].wait()
        by_block(g, qs)
        go_loads += [load(go_ref, g, loc_sem.at[9 + g])]
    keys.second()
    for g in range(KVH):
        go_loads[g].wait()
        by_block(g, gos)

    def take_keys(q):
        for core in range(2):
            s = q * 2 + core
            extra = ka[s, ROWS:, 0:384].astype(F32)
            block_s, label_s, seg_s = extra[:, 0:128], extra[:, 128:256], extra[:, 256:384]
            rank = ranks_of(block_s)
            base = block_s[0:1] * SLOTS
            main = jnp.where(rank < 8.0, base + core * 8 + rank, -1.0)
            slot8 = (lax.rem(s, 8) * 2).astype(F32)
            over = jnp.where(rank < 8.0, -1.0, base + slot8 + rank - 8.0)
            hot = (rows256 == main).astype(F32)
            sel[q, :, core * ROWS : (core + 1) * ROWS] = hot.astype(BF16)
            hot_over = (rows256 == over).astype(F32)
            lanes = pl.ds(pl.multiple_of(lax.rem(s, 8) * ROWS, ROWS), ROWS)
            selo[s // 8, :, lanes] = hot_over.astype(BF16)
            marks = dot((hot * label_s[0:1]).astype(BF16), ones)
            marks = marks if core == 0 else marks + before
            before = marks
            labo[s // 8] += dot((hot_over * label_s[0:1]).astype(BF16), ones)
            mine = (low4 + (s * SLOTS).astype(F32) == own_slot).astype(F32)
            columns = dot((mine * label[0:1]).astype(BF16), ones)
            at_row = (columns == lane1).astype(F32).astype(BF16)
            posl[s] = dot_nt(label.astype(BF16), mine.astype(BF16))
            startl[s] = dot_nt(seg_s.astype(BF16), at_row) + 1.0
        labk[:, q] = marks.astype(BF16).reshape(RANKS, SLOTS, ROWS)
        take_pair(ka, xa, q)

    def take_pair(buf, dst, q):
        pair = buf[pl.ds(q * 2, 2), 0:ROWS, :].reshape(2 * ROWS, KVW)
        dst[:, q] = dot(sel[q], pair).astype(BF16).reshape(RANKS, SLOTS, KVW)

    def take_over(buf, dst):
        for half in range(2):
            rows = buf[half * 8 : half * 8 + 8, 0:ROWS, :].reshape(8 * ROWS, KVW)
            dst[:, 8 + half] = dot(selo[half], rows).astype(BF16).reshape(RANKS, SLOTS, KVW)

    labo[...] = jnp.zeros_like(labo)
    keys.take((0,), take_keys)
    keys.third()
    keys.take((1, 2, 3), take_keys)
    keys.fourth()
    keys.take((4, 5, 6, 7), take_keys)
    take_over(ka, xa)
    for half in range(2):
        labk[:, 8 + half] = labo[half].astype(BF16).reshape(RANKS, SLOTS, ROWS)

    def first_pass(t, _):
        marks = labk[t].reshape(KEYS, ROWS).astype(F32)
        bias = jnp.where((marks <= posl[t][0:1]) & (marks >= startl[t][0:1]), 0.0, -1e30)
        for g in range(KVH):
            cols = slice(g * HD, (g + 1) * HD)
            scores = dot_nt(xa[t, :, :, cols].reshape(KEYS, HD), qs[t, g]) * (INV_ROOT * LOG2E) + bias
            peak = jnp.maximum(jnp.max(scores, axis=0, keepdims=True), -1e29)
            expo = jnp.exp2(scores - peak)
            total = jnp.maximum(jnp.sum(expo, axis=0, keepdims=True), 0.5)
            low = (expo * (1.0 / total)).astype(BF16)
            probs[t, g] = low
            xb[t, :, :, cols] = dot(low, gos[t, g]).astype(BF16).reshape(10, SLOTS, HD)
        return 0

    lax.fori_loop(0, 4, first_pass, 0)

    for e in li_own:
        e.wait()
    w_own.wait()
    for r in li_copies:
        r.wait_recv()
    w_copy.wait_recv()

    def value_term(core):
        def chunk(n, _):
            cols = pl.ds(pl.multiple_of(n * 256, 256), 256)
            part = dot(li[0, pl.ds(core * 4, 4)].reshape(HALF, HALF), wm[0, :, cols])
            part += dot(li[1, pl.ds(core * 4, 4)].reshape(HALF, HALF), wm[1, :, cols])
            vp[pl.ds(core * 4, 4), :, cols] = part.astype(BF16).reshape(4, ROWS, 256)
            return 0

        lax.fori_loop(0, 4, chunk, 0)

    value_term(1 - c)
    v_sib = remote(vp.at[pl.ds((1 - c) * 4, 4)], vsib, vs_sem.at[0], vs_sem.at[1], sib)
    v_sib.start()
    value_term(c)
    lax.fori_loop(4, 6, first_pass, 0)

    v_sib.wait_recv()
    vx = []
    own_v = None
    for o, dx in enumerate((2, 1, 3)):
        tx = lax.rem(x + dx, 4)
        vp[c * 4 + tx] = (vp[c * 4 + tx].astype(F32) + vsib[tx].astype(F32)).astype(BF16)
        r = remote(
            vp.at[c * 4 + tx], vrow.at[o], vx_sem.at[0, o], vx_sem.at[1, o],
            device(y, zl, c, zh, tx),
        )
        r.start()
        vx += [r]
    lax.fori_loop(6, 16, first_pass, 0)
    keys.drain()

    class Scatter:
        def __init__(self, sb, rb, ssems, rsems):
            self.sb, self.rb = sb, rb
            self.twin = [
                remote(self.block(q, 1 - c), sb.at[q], ssems.at[0, q], ssems.at[1, q], sib)
                for q in range(8)
            ]
            oz = 1 - zl
            plan = (
                (y_far * 2 + oz, 0, 0, ROWS, dev_z), (y_up * 2 + oz, 1, 0, ROWS, dev_up),
                (y_down * 2 + oz, 2, 0, ROWS, dev_down),
                (y_far * 2 + zl, 3, 0, 64, dev_up), (y_far * 2 + zl, 3, 64, 64, dev_down),
                (y * 2 + oz, 4, 0, ROWS, dev_z),
                (y_up * 2 + zl, 5, 0, ROWS, dev_up), (y_down * 2 + zl, 6, 0, ROWS, dev_down),
            )
            self.hops = [
                remote(
                    ka.at[c * 8 + q, pl.ds(first, count)], rb.at[slot, pl.ds(first, count)],
                    rsems.at[0, i], rsems.at[1, i], dev,
                )
                for i, (q, slot, first, count, dev) in enumerate(plan)
            ]

        def block(self, q, core):
            return ka.at[core * 8 + q, pl.ds(0, ROWS)]

        def part(self, q, core):
            s = q * 2 + core
            lanes = pl.ds(pl.multiple_of(core * ROWS, ROWS), ROWS)
            total = dot_tn(sel[q, :, lanes], xb[:, q].reshape(256, KVW))
            lanes = pl.ds(pl.multiple_of(lax.rem(s, 8) * ROWS, ROWS), ROWS)
            return total + dot_tn(selo[s // 8, :, lanes], xb[:, 8 + s // 8].reshape(256, KVW))

        def start(self):
            for q in range(8):
                ka[(1 - c) * 8 + q, 0:ROWS, :] = self.part(q, 1 - c).astype(BF16)
                self.twin[q].start()

        def join(self, q):
            total = self.part(q, c) + self.sb[q].astype(F32)
            ka[c * 8 + q, 0:ROWS, :] = total.astype(BF16)

        def first(self):
            for r in self.twin:
                r.wait_recv()
            oz = 1 - zl
            for i, q in enumerate((y_far * 2 + oz, y_up * 2 + oz, y_down * 2 + oz)):
                self.join(q)
                self.hops[i].start()
            for q in (y_far * 2 + zl, y * 2 + oz, y_up * 2 + zl, y_down * 2 + zl, y * 2 + zl):
                self.join(q)

        def add(self, q, slots, first=0, count=ROWS):
            at = (c * 8 + q, slice(first, first + count))
            total = ka[at].astype(F32)
            for slot in slots:
                total = total + self.rb[slot, first : first + count].astype(F32)
            ka[at] = total.astype(BF16)

        def second(self):
            self.hops[0].wait_recv()
            self.add(y_far * 2 + zl, (0,))
            self.hops[3].start()
            self.hops[4].start()
            self.hops[1].wait_recv()
            self.hops[2].wait_recv()
            self.add(y * 2 + 1 - zl, (1, 2))
            self.hops[5].start()

        def third(self):
            self.hops[3].wait_recv()
            self.add(y_up * 2 + zl, (3,), 0, 64)
            self.hops[6].start()
            self.hops[4].wait_recv()
            self.add(y_down * 2 + zl, (3,), 64, 64)
            self.hops[7].start()

        def finish(self):
            for i in (5, 6, 7):
                self.hops[i].wait_recv()
            total = ka[c * 8 + y * 2 + zl, 0:ROWS].astype(F32)
            for slot in (4, 5, 6):
                total = total + self.rb[slot].astype(F32)
            return total.astype(BF16)

        def drain(self):
            for r in self.hops + self.twin:
                r.wait_send()

    grads = Scatter(sb1, rb1, s1_sem, r1_sem)
    grads.start()
    vsum = vp[c * 4 + x].astype(F32) + vsib[x].astype(F32)
    for o in range(3):
        vx[o].wait_recv()
        vsum = vsum + vrow[o].astype(F32)
    va[d] = vsum.astype(BF16)
    vals = Gather(va, ROWS, v_sem, vf_sem)
    grads.first()
    vals.start()
    grads.second()
    vals.second()
    grads.third()
    vals.third()
    gva[me_line] = grads.finish()

    gx = []
    gf = []
    for o, dx in enumerate((2, 1, 3)):
        r = remote(
            gva.at[me_line], gva.at[me_line], gx_sem.at[0, o], gx_sem.at[1, o],
            device(y, zl, c, zh, lax.rem(x + dx, 4)),
        )
        r.start()
        gx += [r]
    r = remote(gva.at[me_line], gva.at[me_line], gf_sem.at[0, 3], gf_sem.at[1, 3], sib)
    r.start()
    gf += [r]

    def take_values(q):
        take_pair(va, xb, q)

    vals.take((0, 1, 2, 3), take_values)
    vals.fourth()
    vals.take((4, 5, 6, 7), take_values)
    take_over(va, xb)

    def second_pass(t, _):
        for g in range(KVH):
            cols = slice(g * HD, (g + 1) * HD)
            grad_probs = dot_nt(xb[t, :, :, cols].reshape(KEYS, HD), gos[t, g])
            low = probs[t, g].astype(F32)
            row_dots = jnp.sum(low * grad_probs, axis=0, keepdims=True)
            grad_scores = (low * (grad_probs - row_dots)).astype(BF16)
            key_part = dot(grad_scores, qs[t, g]) * INV_ROOT
            xb[t, :, :, cols] = key_part.astype(BF16).reshape(10, SLOTS, HD)
            query_part = dot_tn(grad_scores, xa[t, :, :, cols].reshape(KEYS, HD)) * INV_ROOT
            qs[t, g] = query_part.astype(BF16)
        return 0

    lax.fori_loop(0, 4, second_pass, 0)
    for o, dx in enumerate((2, 1, 3)):
        src = c * 4 + lax.rem(x - dx + 4, 4)
        gx[o].wait_recv()
        r = remote(gva.at[src], gva.at[src], gf_sem.at[0, o], gf_sem.at[1, o], sib)
        r.start()
        gf += [r]
    for r in vx + [v_sib]:
        r.wait_send()
    lax.fori_loop(4, 6, second_pass, 0)
    for r in gf:
        r.wait_recv()

    def input_term(n, _):
        h, first = n // 2, pl.multiple_of(lax.rem(n, 2) * 256, 256)
        part = dot_nt(gva[...].reshape(1024, KVW), wm[h, pl.ds(first, 256), :])
        cols = pl.ds(pl.multiple_of(n * 256, 256), 256)
        vp[:, :, cols] = part.astype(BF16).reshape(8, ROWS, 256)
        return 0

    lax.fori_loop(0, 4, input_term, 0)
    gi_cols = [pl.ds(pl.multiple_of(h * 4096 + x * 1024 + c * HALF, HALF), HALF) for h in range(2)]
    gi_copies = []
    gi_own = []
    for o, step in enumerate(LINE_STEPS):
        tx, tc = line_at(step)
        for h in range(2):
            r = remote(
                vp.at[tc * 4 + tx, :, pl.ds(h * HALF, HALF)], gi_ref.at[:, gi_cols[h]],
                gi_sem.at[0, o * 2 + h], gi_sem.at[1, o * 2 + h], line_dev(step),
            )
            r.start()
            gi_copies += [r]
    for h in range(2):
        e = pltpu.make_async_copy(
            vp.at[me_line, :, pl.ds(h * HALF, HALF)], gi_ref.at[:, gi_cols[h]], loc_sem.at[20 + h]
        )
        e.start()
        gi_own += [e]

    for h in range(2):
        for n in range(4):
            part = dot_tn(
                li[h].reshape(1024, HALF), gva[:, :, n * 256 : (n + 1) * 256].reshape(1024, 256)
            )
            part = part.astype(BF16).reshape(8, 64, 256)
            cols = slice((n % 2) * 256, (n % 2) * 256 + 256)
            for fb in range(8):
                zt, x1, x0 = fb // 4, (fb // 2) % 2, fb % 2
                if n < 2:
                    ga[zt * 2 + x0, h * 2 + x1, :, cols] = part[fb]
                else:
                    gb[h * 2 + x1, zt * 2 + x0, :, cols] = part[fb]
    g1 = []
    for i in range(3):
        r = remote(ga.at[lax.rem(z + i + 1, 4)], ra.at[i], g1_sem.at[0, i], g1_sem.at[1, i], z_devs[i])
        r.start()
        g1 += [r]
        r = remote(
            gb.at[lax.rem(y + i + 1, 4)], rbb.at[i], g1_sem.at[0, 3 + i], g1_sem.at[1, 3 + i], y_devs[i]
        )
        r.start()
        g1 += [r]

    lax.fori_loop(6, 11, second_pass, 0)
    for r in g1:
        r.wait_recv()
    ga[z] = (
        ga[z].astype(F32) + ra[0].astype(F32) + ra[1].astype(F32) + ra[2].astype(F32)
    ).astype(BF16)
    gb[y] = (
        gb[y].astype(F32) + rbb[0].astype(F32) + rbb[1].astype(F32) + rbb[2].astype(F32)
    ).astype(BF16)

    def owners():
        for i in range(4):
            h, x1 = i // 2, i % 2
            ty, tx = 2 * h + x // 2, x1 * 2 + zl
            yield (
                in_own_line & (ty == y) & (tx == x), device(ty, lax.rem(x, 2), c, zh, tx),
                ga.at[z, i], gwa.at[y], g2s_sem.at[i], g2r_sem.at[y],
            )
            zt, x0 = i // 2, i % 2
            ty, tx = 2 * (y // 2) + x // 2, lax.rem(y, 2) * 2 + x0
            yield (
                in_own_line & (zt == zh) & (tx == x), device(ty, lax.rem(x, 2), c, zt, tx),
                gb.at[y, i], gwb.at[z], g2s_sem.at[4 + i], g2r_sem.at[4 + z],
            )

    for to_self, dev, src, dst, ssem, rsem in owners():

        @pl.when(to_self)
        def _():
            pltpu.make_async_copy(src, dst, rsem).start()

        @pl.when(jnp.logical_not(to_self))
        def _():
            remote(src, dst, ssem, rsem, dev).start()

    lax.fori_loop(11, 16, second_pass, 0)
    grads.drain()
    vals.drain()
    last = Scatter(sb2, rb2, s2_sem, r2_sem)
    last.start()
    last.first()

    q_out = []
    for g in range(KVH):
        if g == 3:
            last.second()
        if g == 6:
            last.third()
        slots = jnp.concatenate(
            [qs[:, g, h * SLOTS : (h + 1) * SLOTS, :].reshape(256, HD) for h in range(GROUP)], axis=1
        )
        va[g] = dot_tn(own_sel, slots).astype(BF16)
        e = pltpu.make_async_copy(va.at[g], gq_ref.at[:, pl.ds(g * 1024, 1024)], out_sem.at[g])
        e.start()
        q_out += [e]

    for i in range(4):
        pltpu.make_async_copy(gwa.at[i], gwa.at[i], g2r_sem.at[i]).wait()
        pltpu.make_async_copy(gwb.at[i], gwb.at[i], g2r_sem.at[4 + i]).wait()
    gw_ref[:, 0:HALF] = (gwa[0].astype(F32) + gwa[1].astype(F32)) + (gwa[2].astype(F32) + gwa[3].astype(F32))
    gw_ref[:, HALF:] = (gwb[0].astype(F32) + gwb[1].astype(F32)) + (gwb[2].astype(F32) + gwb[3].astype(F32))
    gk_ref[...] = last.finish()

    for r in gi_copies:
        r.wait()
    for e in gi_own + q_out:
        e.wait()
    for r in li_copies + [w_copy] + gx + gf + g1:
        r.wait_send()
    last.drain()
    for to_self, dev, src, dst, ssem, rsem in owners():

        @pl.when(jnp.logical_not(to_self))
        def _():
            remote(src, dst, ssem, rsem, dev).wait_send()


def shards(layer_input, queries, key_rows, grad_out, w_value, destination, seg_start):
    any_spec = pl.BlockSpec(memory_space=pl.ANY)
    vmem_spec = pl.BlockSpec(memory_space=pltpu.VMEM)
    dma = pltpu.SemaphoreType.DMA
    tokens = pltpu.VMEM
    return pl.pallas_call(
        kernel,
        out_shape=(
            jax.ShapeDtypeStruct(queries.shape, BF16),
            jax.ShapeDtypeStruct(key_rows.shape, BF16),
            jax.ShapeDtypeStruct(layer_input.shape, BF16),
            jax.ShapeDtypeStruct((64, KVW), F32),
        ),
        in_specs=[any_spec] * 5 + [vmem_spec] * 2,
        out_specs=(any_spec, vmem_spec, any_spec, vmem_spec),
        scratch_shapes=[
            tokens((RANKS, ROWS + SLOTS, KVW), BF16),
            tokens((RANKS, ROWS, KVW), BF16),
            tokens((RANKS, KVH, ROWS, HD), BF16),
            tokens((RANKS, KVH, ROWS, HD), BF16),
            tokens((RANKS, 10, SLOTS, KVW), BF16),
            tokens((RANKS, 10, SLOTS, KVW), BF16),
            tokens((RANKS, KVH, KEYS, ROWS), BF16),
            tokens((2, 8, ROWS, HALF), BF16),
            tokens((2, HALF, KVW), BF16),
            tokens((8, ROWS, KVW), BF16),
            tokens((4, ROWS, KVW), BF16),
            tokens((3, ROWS, KVW), BF16),
            tokens((8, ROWS, KVW), BF16),
            tokens((7, ROWS, KVW), BF16),
            tokens((8, ROWS, KVW), BF16),
            tokens((7, ROWS, KVW), BF16),
            tokens((8, ROWS, KVW), BF16),
            tokens((4, 4, 64, HALF), BF16),
            tokens((4, 4, 64, HALF), BF16),
            tokens((3, 4, 64, HALF), BF16),
            tokens((3, 4, 64, HALF), BF16),
            tokens((4, 64, HALF), BF16),
            tokens((4, 64, HALF), BF16),
            tokens((8, 256, 256), BF16),
            tokens((2, 256, 1024), BF16),
            tokens((RANKS, 10, SLOTS, ROWS), BF16),
            tokens((2, 256, ROWS), F32),
            tokens((RANKS, SLOTS, ROWS), F32),
            tokens((RANKS, SLOTS, ROWS), F32),
            dma((22,)),
            dma((2, 8)),
            dma((2, 8)),
            dma((2, 8)),
            dma((2, 8)),
            dma((2, 14)),
            dma((2,)),
            dma((2,)),
            dma((2, 3)),
            dma((2, 8)),
            dma((2, 8)),
            dma((2, 8)),
            dma((2, 8)),
            dma((2, 3)),
            dma((2, 4)),
            dma((2, 14)),
            dma((2, 6)),
            dma((8,)),
            dma((8,)),
            dma((8,)),
        ],
        name="packed_backward",
        compiler_params=pltpu.CompilerParams(
            collective_id=0, has_side_effects=True, vmem_limit_bytes=64 * 1024 * 1024
        ),
    )(
        layer_input, queries, key_rows, grad_out, w_value,
        destination.reshape(1, ROWS), seg_start.reshape(1, ROWS),
    )


def solution(mesh):
    both = P(("dp", "fsdp"), None)
    return jax.shard_map(
        shards,
        mesh=mesh,
        in_specs=(both, both, both, both, P("fsdp", None), P(("dp", "fsdp")), P(("dp", "fsdp"))),
        out_specs=(both, both, both, both),
        check_vma=False,
    )
```

```python
import functools

import jax
import jax.numpy as jnp
from jax import lax
from jax.experimental import pallas as pl
from jax.experimental.pallas import tpu as pltpu
from jax.sharding import PartitionSpec as P

MESH = pl.DeviceIdType.MESH
F32 = jnp.float32
BF16 = jnp.bfloat16
HD = 128
ROWS = 128
RANKS = 16
SLOTS = 16
KVH = 8
GROUP = 8
KVW = KVH * HD
HALF = 512
KEYS = 160
INV_ROOT = 1.0 / HD**0.5
LOG2E = 1.4426950408889634
LINE_STEPS = ((1, 0), (3, 0), (1, 1), (3, 1), (2, 0), (2, 1), (0, 1))


def dot(a, b):
    return jnp.dot(a, b, preferred_element_type=F32)


def dot_nt(a, b):
    return lax.dot_general(a, b, (((1,), (1,)), ((), ())), preferred_element_type=F32)


def dot_tn(a, b):
    return lax.dot_general(a, b, (((0,), (0,)), ((), ())), preferred_element_type=F32)


def device(y, zl, c, zh, x):
    return (y * 4 + zl * 2 + c, zh * 4 + x)


def kernel(
    li_ref, q_ref, k_ref, go_ref, w_ref, dest_ref, seg_ref,
    gq_ref, gk_ref, gi_ref, gw_ref,
    ka, va, qs, gos, xa, xb, probs, li, wm, vp, vsib, vrow, sb1, rb1, sb2, rb2, gva,
    ga, gb, ra, rbb, gwa, gwb, sel, selo, labk, labo, posl, startl,
    loc_sem, k_sem, kf_sem, v_sem, vf_sem, li_sem, w_sem, vs_sem, vx_sem,
    s1_sem, r1_sem, s2_sem, r2_sem, gx_sem, gf_sem, gi_sem, g1_sem, g2s_sem, g2r_sem, out_sem,
):
    d, f = lax.axis_index("dp"), lax.axis_index("fsdp")
    y, zl, c = d // 4, lax.rem(d // 2, 2), lax.rem(d, 2)
    zh, x = f // 4, lax.rem(f, 4)
    z = zh * 2 + zl
    sib = device(y, zl, 1 - c, zh, x)
    y_up, y_down, y_far = lax.rem(y + 1, 4), lax.rem(y + 3, 4), lax.rem(y + 2, 4)
    dev_up, dev_down = device(y_up, zl, c, zh, x), device(y_down, zl, c, zh, x)
    dev_z = device(y, 1 - zl, c, zh, x)

    def line_at(step, sign=1):
        return lax.rem(x + sign * step[0] + 4, 4), lax.rem(c + step[1], 2)

    def line_dev(step, sign=1):
        tx, tc = line_at(step, sign)
        return device(y, zl, tc, zh, tx)

    def remote(src, dst, ssem, rsem, dev):
        return pltpu.make_async_remote_copy(
            src_ref=src, dst_ref=dst, send_sem=ssem, recv_sem=rsem, device_id=dev, device_id_type=MESH
        )

    own_k = pltpu.make_async_copy(k_ref, ka.at[d, pl.ds(0, ROWS)], loc_sem.at[0])
    own_k.start()

    def load(ref, g, sem):
        e = pltpu.make_async_copy(ref.at[:, pl.ds(g * 1024, 1024)], vp.at[g], sem)
        e.start()
        return e

    q_loads = [load(q_ref, g, loc_sem.at[1 + g]) for g in range(KVH)]
    me_line = c * 4 + x
    li_own = []
    for h in range(2):
        e = pltpu.make_async_copy(
            li_ref.at[:, pl.ds(pl.multiple_of(h * 4096 + x * 1024 + c * HALF, HALF), HALF)],
            li.at[h, me_line],
            loc_sem.at[17 + h],
        )
        e.start()
        li_own += [e]
    own_rows = w_ref.at[pl.ds(pl.multiple_of(c * HALF, HALF), HALF)]
    w_own = pltpu.make_async_copy(own_rows, wm.at[zh], loc_sem.at[19])
    w_own.start()

    barrier = pltpu.get_barrier_semaphore()

    def greet(dev):
        pl.semaphore_signal(barrier, inc=1, device_id=dev, device_id_type=MESH)

    w_dev = device(y, 1 - zl, c, 1 - zh, x)
    z_devs = [device(y, lax.rem(z + i, 2), c, lax.rem(z + i, 4) // 2, x) for i in (1, 2, 3)]
    y_devs = [device(lax.rem(y + i, 4), zl, c, zh, x) for i in (1, 2, 3)]
    x_src = lax.rem(y, 2) * 2 + zl
    in_own_line = x == x_src
    for dev in [dev_up, dev_down, dev_z, w_dev] + z_devs + y_devs:
        greet(dev)
    for step in LINE_STEPS:
        greet(line_dev(step, -1))
    y_src = 2 * (y // 2) + x // 2
    for i in range(4):

        @pl.when(jnp.logical_not(in_own_line & (y == i) & (zl == lax.rem(x, 2))))
        def _():
            greet(device(i, lax.rem(x, 2), c, zh, x_src))

        @pl.when(jnp.logical_not(in_own_line & (y == y_src) & (z == i)))
        def _():
            greet(device(y_src, i % 2, c, i // 2, x_src))

    pl.semaphore_wait(barrier, 10 + 7 + 8 - 2 * in_own_line.astype(jnp.int32))

    dest = jnp.broadcast_to(dest_ref[...], (SLOTS, ROWS))
    block = (dest >> 7).astype(F32)
    label = (dest & 127).astype(F32) + 1.0
    seg = jnp.broadcast_to(seg_ref[...], (SLOTS, ROWS)).astype(F32)
    ka[d, ROWS:, :] = jnp.concatenate(
        [block, label, seg] + [jnp.zeros((SLOTS, ROWS), F32)] * 5, axis=1
    ).astype(BF16)
    own_k.wait()

    class Gather:
        def __init__(self, buf, rows, sems, fsems):
            chips = [(y, zl), (y, 1 - zl), (y_down, zl), (y_up, zl)]
            chips += [(y_down, 1 - zl), (y_up, 1 - zl), (y_far, zl), (y_far, 1 - zl)]
            self.q = [cy * 2 + cz for cy, cz in chips]
            me, zs, yd, yu, _, _, yo, _ = [q * 2 + c for q in self.q]

            def hop(i, slot, dev, first=0, count=rows):
                part = buf.at[slot, pl.ds(first, count)]
                return remote(part, part, sems.at[0, i], sems.at[1, i], dev)

            self.hops = [
                hop(0, me, dev_up), hop(1, me, dev_down), hop(2, me, dev_z),
                hop(3, zs, dev_up), hop(4, zs, dev_down),
                hop(5, yd, dev_up, 0, 64), hop(6, yu, dev_down, 64, rows - 64),
                hop(7, yo, dev_z),
            ]
            self.twin = [
                remote(buf.at[q * 2 + c], buf.at[q * 2 + c], fsems.at[0, j], fsems.at[1, j], sib)
                for j, q in enumerate(self.q)
            ]

        def start(self):
            for r in self.hops[:3] + self.twin[:1]:
                r.start()

        def second(self):
            hops, twin = self.hops, self.twin
            hops[2].wait_recv()
            for r in (hops[3], hops[4], twin[1]):
                r.start()
            hops[0].wait_recv()
            for r in (hops[5], twin[2]):
                r.start()
            hops[1].wait_recv()
            for r in (hops[6], twin[3]):
                r.start()

        def third(self):
            hops, twin = self.hops, self.twin
            hops[5].wait_recv()
            hops[6].wait_recv()
            for r in (hops[7], twin[6]):
                r.start()
            hops[3].wait_recv()
            twin[4].start()
            hops[4].wait_recv()
            twin[5].start()

        def fourth(self):
            self.hops[7].wait_recv()
            self.twin[7].start()

        def take(self, which, taker):
            for j in which:
                self.twin[j].wait_recv()
                taker(self.q[j])

        def drain(self):
            for r in self.hops + self.twin:
                r.wait_send()

    keys = Gather(ka, ROWS + SLOTS, k_sem, kf_sem)
    keys.start()
    li_copies = []
    for o, step in enumerate(LINE_STEPS):
        tx, tc = line_at(step)
        for h in range(2):
            r = remote(
                li_ref.at[:, pl.ds(pl.multiple_of(h * 4096 + tx * 1024 + tc * HALF, HALF), HALF)],
                li.at[h, me_line],
                li_sem.at[0, o * 2 + h],
                li_sem.at[1, o * 2 + h],
                line_dev(step),
            )
            r.start()
            li_copies += [r]
    w_copy = remote(own_rows, wm.at[zh], w_sem.at[0], w_sem.at[1], w_dev)
    w_copy.start()

    rows16 = lax.broadcasted_iota(jnp.int32, (SLOTS, ROWS), 0).astype(F32)
    tri = (
        lax.broadcasted_iota(jnp.int32, (ROWS, ROWS), 0)
        < lax.broadcasted_iota(jnp.int32, (ROWS, ROWS), 1)
    ).astype(F32).astype(BF16)
    ones = jnp.ones((ROWS, ROWS), BF16)
    rows256 = lax.broadcasted_iota(jnp.int32, (256, ROWS), 0).astype(F32)
    lane1 = lax.broadcasted_iota(jnp.int32, (ROWS, ROWS), 1).astype(F32) + 1.0
    low4 = (lax.broadcasted_iota(jnp.int32, (ROWS, ROWS), 0) & 15).astype(F32)

    def ranks_of(block16):
        hot = (block16 == rows16).astype(F32)
        return jnp.sum(hot * dot(hot.astype(BF16), tri), axis=0, keepdims=True)

    own_slot = block[0:1] * SLOTS + ranks_of(block)
    own_sel = (rows256 == own_slot).astype(F32).astype(BF16)

    def by_block(g, dst):
        placed = dot(own_sel, vp[g]).astype(BF16)
        for h in range(GROUP):
            dst[:, g, h * SLOTS : (h + 1) * SLOTS, :] = placed[:, h * HD : (h + 1) * HD].reshape(
                RANKS, SLOTS, HD
            )

    go_loads = []
    for g in range(KVH):
        q_loads[g].wait()
        by_block(g, qs)
        go_loads += [load(go_ref, g, loc_sem.at[9 + g])]
    keys.second()
    for g in range(KVH):
        go_loads[g].wait()
        by_block(g, gos)

    def take_keys(q):
        for core in range(2):
            s = q * 2 + core
            extra = ka[s, ROWS:, 0:384].astype(F32)
            block_s, label_s, seg_s = extra[:, 0:128], extra[:, 128:256], extra[:, 256:384]
            rank = ranks_of(block_s)
            base = block_s[0:1] * SLOTS
            main = jnp.where(rank < 8.0, base + core * 8 + rank, -1.0)
            slot8 = (lax.rem(s, 8) * 2).astype(F32)
            over = jnp.where(rank < 8.0, -1.0, base + slot8 + rank - 8.0)
            hot = (rows256 == main).astype(F32)
            sel[q, :, core * ROWS : (core + 1) * ROWS] = hot.astype(BF16)
            hot_over = (rows256 == over).astype(F32)
            lanes = pl.ds(pl.multiple_of(lax.rem(s, 8) * ROWS, ROWS), ROWS)
            selo[s // 8, :, lanes] = hot_over.astype(BF16)
            marks = dot((hot * label_s[0:1]).astype(BF16), ones)
            marks = marks if core == 0 else marks + before
            before = marks
            labo[s // 8] += dot((hot_over * label_s[0:1]).astype(BF16), ones)
            mine = (low4 + (s * SLOTS).astype(F32) == own_slot).astype(F32)
            columns = dot((mine * label[0:1]).astype(BF16), ones)
            at_row = (columns == lane1).astype(F32).astype(BF16)
            posl[s] = dot_nt(label.astype(BF16), mine.astype(BF16))
            startl[s] = dot_nt(seg_s.astype(BF16), at_row) + 1.0
        labk[:, q] = marks.astype(BF16).reshape(RANKS, SLOTS, ROWS)
        take_pair(ka, xa, q)

    def take_pair(buf, dst, q):
        pair = buf[pl.ds(q * 2, 2), 0:ROWS, :].reshape(2 * ROWS, KVW)
        dst[:, q] = dot(sel[q], pair).astype(BF16).reshape(RANKS, SLOTS, KVW)

    def take_over(buf, dst):
        for half in range(2):
            rows = buf[half * 8 : half * 8 + 8, 0:ROWS, :].reshape(8 * ROWS, KVW)
            dst[:, 8 + half] = dot(selo[half], rows).astype(BF16).reshape(RANKS, SLOTS, KVW)

    labo[...] = jnp.zeros_like(labo)
    keys.take((0,), take_keys)
    keys.third()
    keys.take((1, 2, 3), take_keys)
    keys.fourth()
    keys.take((4, 5, 6, 7), take_keys)
    take_over(ka, xa)
    for half in range(2):
        labk[:, 8 + half] = labo[half].astype(BF16).reshape(RANKS, SLOTS, ROWS)

    def first_pass(half, first, last):
        def block_step(t, _):
            marks = labk[t].reshape(KEYS, ROWS).astype(F32)
            bias = jnp.where((marks <= posl[t][0:1]) & (marks >= startl[t][0:1]), 0.0, -1e30)
            heads = range(half * 4, half * 4 + 4)
            cols = [slice(g * HD, (g + 1) * HD) for g in heads]
            scores = [dot_nt(xa[t, :, :, at].reshape(KEYS, HD), qs[t, g]) for g, at in zip(heads, cols)]
            scores = [v * (INV_ROOT * LOG2E) + bias for v in scores]
            peaks = [jnp.maximum(jnp.max(v, axis=0, keepdims=True), -1e29) for v in scores]
            expos = [jnp.exp2(v - peak) for v, peak in zip(scores, peaks)]
            totals = [jnp.maximum(jnp.sum(v, axis=0, keepdims=True), 0.5) for v in expos]
            lows = [(v * (1.0 / total)).astype(BF16) for v, total in zip(expos, totals)]
            parts = [dot(low, gos[t, g]).astype(BF16) for g, low in zip(heads, lows)]
            for g, at, low, part in zip(heads, cols, lows, parts):
                probs[t, g] = low
                xb[t, :, :, at] = part.reshape(10, SLOTS, HD)
            return 0

        lax.fori_loop(first, last, block_step, 0)

    first_pass(0, 0, 6)

    for e in li_own:
        e.wait()
    w_own.wait()
    for r in li_copies:
        r.wait_recv()
    w_copy.wait_recv()

    def value_term(core):
        def chunk(n, _):
            cols = pl.ds(pl.multiple_of(n * 256, 256), 256)
            part = dot(li[0, pl.ds(core * 4, 4)].reshape(HALF, HALF), wm[0, :, cols])
            part += dot(li[1, pl.ds(core * 4, 4)].reshape(HALF, HALF), wm[1, :, cols])
            vp[pl.ds(core * 4, 4), :, cols] = part.astype(BF16).reshape(4, ROWS, 256)
            return 0

        lax.fori_loop(0, 4, chunk, 0)

    value_term(1 - c)
    v_sib = remote(vp.at[pl.ds((1 - c) * 4, 4)], vsib, vs_sem.at[0], vs_sem.at[1], sib)
    v_sib.start()
    value_term(c)
    first_pass(0, 6, 16)

    v_sib.wait_recv()
    vx = []
    own_v = None
    for o, dx in enumerate((2, 1, 3)):
        tx = lax.rem(x + dx, 4)
        vp[c * 4 + tx] = (vp[c * 4 + tx].astype(F32) + vsib[tx].astype(F32)).astype(BF16)
        r = remote(
            vp.at[c * 4 + tx], vrow.at[o], vx_sem.at[0, o], vx_sem.at[1, o],
            device(y, zl, c, zh, tx),
        )
        r.start()
        vx += [r]
    keys.drain()

    class Scatter:
        def __init__(self, half, sb, rb, ssems, rsems):
            self.sb, self.rb = sb, rb
            self.cols = slice(half * HALF, (half + 1) * HALF)
            lanes = pl.ds(half * HALF, HALF)
            base = half * 2
            self.twin = [
                remote(
                    ka.at[(1 - c) * 8 + q, pl.ds(0, ROWS), lanes], sb.at[q, :, lanes],
                    ssems.at[base, q], ssems.at[base + 1, q], sib,
                )
                for q in range(8)
            ]
            oz = 1 - zl
            plan = (
                (y_far * 2 + oz, 0, 0, ROWS, dev_z), (y_up * 2 + oz, 1, 0, ROWS, dev_up),
                (y_down * 2 + oz, 2, 0, ROWS, dev_down),
                (y_far * 2 + zl, 3, 0, 64, dev_up), (y_far * 2 + zl, 3, 64, 64, dev_down),
                (y * 2 + oz, 4, 0, ROWS, dev_z),
                (y_up * 2 + zl, 5, 0, ROWS, dev_up), (y_down * 2 + zl, 6, 0, ROWS, dev_down),
            )
            self.hops = [
                remote(
                    ka.at[c * 8 + q, pl.ds(first, count), lanes],
                    rb.at[slot, pl.ds(first, count), lanes],
                    rsems.at[base, i], rsems.at[base + 1, i], dev,
                )
                for i, (q, slot, first, count, dev) in enumerate(plan)
            ]

        def part(self, q, core):
            s = q * 2 + core
            lanes = pl.ds(pl.multiple_of(core * ROWS, ROWS), ROWS)
            total = dot_tn(sel[q, :, lanes], xb[:, q, :, self.cols].reshape(256, HALF))
            lanes = pl.ds(pl.multiple_of(lax.rem(s, 8) * ROWS, ROWS), ROWS)
            rows = xb[:, 8 + s // 8, :, self.cols].reshape(256, HALF)
            return total + dot_tn(selo[s // 8, :, lanes], rows)

        def start(self):
            for q in range(8):
                ka[(1 - c) * 8 + q, 0:ROWS, self.cols] = self.part(q, 1 - c).astype(BF16)
                self.twin[q].start()

        def join(self, q):
            total = self.part(q, c) + self.sb[q, :, self.cols].astype(F32)
            ka[c * 8 + q, 0:ROWS, self.cols] = total.astype(BF16)

        def first(self):
            for r in self.twin:
                r.wait_recv()
            oz = 1 - zl
            for i, q in enumerate((y_far * 2 + oz, y_up * 2 + oz, y_down * 2 + oz)):
                self.join(q)
                self.hops[i].start()
            for q in (y_far * 2 + zl, y * 2 + oz, y_up * 2 + zl, y_down * 2 + zl, y * 2 + zl):
                self.join(q)

        def add(self, q, slots, first=0, count=ROWS):
            at = (c * 8 + q, slice(first, first + count), self.cols)
            total = ka[at].astype(F32)
            for slot in slots:
                total = total + self.rb[slot, first : first + count, self.cols].astype(F32)
            ka[at] = total.astype(BF16)

        def second(self):
            self.hops[0].wait_recv()
            self.add(y_far * 2 + zl, (0,))
            self.hops[3].start()
            self.hops[4].start()
            self.hops[1].wait_recv()
            self.hops[2].wait_recv()
            self.add(y * 2 + 1 - zl, (1, 2))
            self.hops[5].start()

        def third(self):
            self.hops[3].wait_recv()
            self.add(y_up * 2 + zl, (3,), 0, 64)
            self.hops[6].start()
            self.hops[4].wait_recv()
            self.add(y_down * 2 + zl, (3,), 64, 64)
            self.hops[7].start()

        def finish(self):
            for i in (5, 6, 7):
                self.hops[i].wait_recv()
            total = ka[c * 8 + y * 2 + zl, 0:ROWS, self.cols].astype(F32)
            for slot in (4, 5, 6):
                total = total + self.rb[slot, :, self.cols].astype(F32)
            return total.astype(BF16)

        def drain(self):
            for r in self.hops + self.twin:
                r.wait_send()

    left = Scatter(0, sb1, rb1, s1_sem, r1_sem)
    right = Scatter(1, sb1, rb1, s1_sem, r1_sem)
    left.start()
    first_pass(1, 0, 6)
    left.first()
    first_pass(1, 6, 12)
    left.second()
    vsum = vp[c * 4 + x].astype(F32) + vsib[x].astype(F32)
    for o in range(3):
        vx[o].wait_recv()
        vsum = vsum + vrow[o].astype(F32)
    va[d] = vsum.astype(BF16)
    vals = Gather(va, ROWS, v_sem, vf_sem)
    vals.start()
    first_pass(1, 12, 16)
    left.third()
    right.start()
    vals.second()
    right.first()
    gva[me_line, :, 0:HALF] = left.finish()
    vals.third()
    right.second()
    right.third()
    gva[me_line, :, HALF:] = right.finish()

    gx = []
    gf = []
    for o, dx in enumerate((2, 1, 3)):
        r = remote(
            gva.at[me_line], gva.at[me_line], gx_sem.at[0, o], gx_sem.at[1, o],
            device(y, zl, c, zh, lax.rem(x + dx, 4)),
        )
        r.start()
        gx += [r]
    r = remote(gva.at[me_line], gva.at[me_line], gf_sem.at[0, 3], gf_sem.at[1, 3], sib)
    r.start()
    gf += [r]

    def take_values(q):
        take_pair(va, xb, q)

    vals.take((0, 1, 2, 3), take_values)
    vals.fourth()
    vals.take((4, 5, 6, 7), take_values)
    take_over(va, xb)

    def second_pass(half, first, last):
        def block_step(t, _):
            heads = range(half * 4, half * 4 + 4)
            cols = [slice(g * HD, (g + 1) * HD) for g in heads]
            grad_probs = [dot_nt(xb[t, :, :, at].reshape(KEYS, HD), gos[t, g]) for g, at in zip(heads, cols)]
            lows = [probs[t, g].astype(F32) for g in heads]
            row_dots = [jnp.sum(low * v, axis=0, keepdims=True) for low, v in zip(lows, grad_probs)]
            grad_scores = [
                (low * (v - dots)).astype(BF16) for low, v, dots in zip(lows, grad_probs, row_dots)
            ]
            key_parts = [dot(v, qs[t, g]) * INV_ROOT for v, g in zip(grad_scores, heads)]
            query_parts = [
                dot_tn(v, xa[t, :, :, at].reshape(KEYS, HD)) * INV_ROOT
                for v, at in zip(grad_scores, cols)
            ]
            for g, at, key_part, query_part in zip(heads, cols, key_parts, query_parts):
                xb[t, :, :, at] = key_part.astype(BF16).reshape(10, SLOTS, HD)
                qs[t, g] = query_part.astype(BF16)
            return 0

        lax.fori_loop(first, last, block_step, 0)

    second_pass(0, 0, 8)
    for o, dx in enumerate((2, 1, 3)):
        src = c * 4 + lax.rem(x - dx + 4, 4)
        gx[o].wait_recv()
        r = remote(gva.at[src], gva.at[src], gf_sem.at[0, o], gf_sem.at[1, o], sib)
        r.start()
        gf += [r]
    for r in vx + [v_sib]:
        r.wait_send()
    second_pass(0, 8, 16)
    left.drain()
    right.drain()
    last_left = Scatter(0, sb2, rb2, s2_sem, r2_sem)
    last_right = Scatter(1, sb2, rb2, s2_sem, r2_sem)
    last_left.start()
    for r in gf:
        r.wait_recv()

    def input_term(n, _):
        h, first = n // 2, pl.multiple_of(lax.rem(n, 2) * 256, 256)
        part = dot_nt(gva[...].reshape(1024, KVW), wm[h, pl.ds(first, 256), :])
        cols = pl.ds(pl.multiple_of(n * 256, 256), 256)
        vp[:, :, cols] = part.astype(BF16).reshape(8, ROWS, 256)
        return 0

    lax.fori_loop(0, 4, input_term, 0)
    gi_cols = [pl.ds(pl.multiple_of(h * 4096 + x * 1024 + c * HALF, HALF), HALF) for h in range(2)]
    gi_copies = []
    gi_own = []
    for o, step in enumerate(LINE_STEPS):
        tx, tc = line_at(step)
        for h in range(2):
            r = remote(
                vp.at[tc * 4 + tx, :, pl.ds(h * HALF, HALF)], gi_ref.at[:, gi_cols[h]],
                gi_sem.at[0, o * 2 + h], gi_sem.at[1, o * 2 + h], line_dev(step),
            )
            r.start()
            gi_copies += [r]
    for h in range(2):
        e = pltpu.make_async_copy(
            vp.at[me_line, :, pl.ds(h * HALF, HALF)], gi_ref.at[:, gi_cols[h]], loc_sem.at[20 + h]
        )
        e.start()
        gi_own += [e]

    last_left.first()

    for h in range(2):
        for n in range(4):
            part = dot_tn(
                li[h].reshape(1024, HALF), gva[:, :, n * 256 : (n + 1) * 256].reshape(1024, 256)
            )
            part = part.astype(BF16).reshape(8, 64, 256)
            cols = slice((n % 2) * 256, (n % 2) * 256 + 256)
            for fb in range(8):
                zt, x1, x0 = fb // 4, (fb // 2) % 2, fb % 2
                if n < 2:
                    ga[zt * 2 + x0, h * 2 + x1, :, cols] = part[fb]
                else:
                    gb[h * 2 + x1, zt * 2 + x0, :, cols] = part[fb]
    g1 = []
    for i in range(3):
        r = remote(ga.at[lax.rem(z + i + 1, 4)], ra.at[i], g1_sem.at[0, i], g1_sem.at[1, i], z_devs[i])
        r.start()
        g1 += [r]
        r = remote(
            gb.at[lax.rem(y + i + 1, 4)], rbb.at[i], g1_sem.at[0, 3 + i], g1_sem.at[1, 3 + i], y_devs[i]
        )
        r.start()
        g1 += [r]

    second_pass(1, 0, 6)
    last_left.second()
    second_pass(1, 6, 12)
    last_left.third()
    for r in g1:
        r.wait_recv()
    ga[z] = (
        ga[z].astype(F32) + ra[0].astype(F32) + ra[1].astype(F32) + ra[2].astype(F32)
    ).astype(BF16)
    gb[y] = (
        gb[y].astype(F32) + rbb[0].astype(F32) + rbb[1].astype(F32) + rbb[2].astype(F32)
    ).astype(BF16)

    def owners():
        for i in range(4):
            h, x1 = i // 2, i % 2
            ty, tx = 2 * h + x // 2, x1 * 2 + zl
            yield (
                in_own_line & (ty == y) & (tx == x), device(ty, lax.rem(x, 2), c, zh, tx),
                ga.at[z, i], gwa.at[y], g2s_sem.at[i], g2r_sem.at[y],
            )
            zt, x0 = i // 2, i % 2
            ty, tx = 2 * (y // 2) + x // 2, lax.rem(y, 2) * 2 + x0
            yield (
                in_own_line & (zt == zh) & (tx == x), device(ty, lax.rem(x, 2), c, zt, tx),
                gb.at[y, i], gwb.at[z], g2s_sem.at[4 + i], g2r_sem.at[4 + z],
            )

    for to_self, dev, src, dst, ssem, rsem in owners():

        @pl.when(to_self)
        def _():
            pltpu.make_async_copy(src, dst, rsem).start()

        @pl.when(jnp.logical_not(to_self))
        def _():
            remote(src, dst, ssem, rsem, dev).start()

    second_pass(1, 12, 16)
    last_right.start()
    vals.drain()

    q_out = []

    def queries_out(g):
        slots = jnp.concatenate(
            [qs[:, g, h * SLOTS : (h + 1) * SLOTS, :].reshape(256, HD) for h in range(GROUP)], axis=1
        )
        va[g] = dot_tn(own_sel, slots).astype(BF16)
        e = pltpu.make_async_copy(va.at[g], gq_ref.at[:, pl.ds(g * 1024, 1024)], out_sem.at[g])
        e.start()
        q_out.append(e)

    for g in range(6):
        queries_out(g)
    last_right.first()
    gk_ref[:, 0:HALF] = last_left.finish()
    queries_out(6)
    queries_out(7)
    last_right.second()
    last_right.third()
    for i in range(4):
        pltpu.make_async_copy(gwa.at[i], gwa.at[i], g2r_sem.at[i]).wait()
        pltpu.make_async_copy(gwb.at[i], gwb.at[i], g2r_sem.at[4 + i]).wait()
    gw_ref[:, 0:HALF] = (gwa[0].astype(F32) + gwa[1].astype(F32)) + (gwa[2].astype(F32) + gwa[3].astype(F32))
    gw_ref[:, HALF:] = (gwb[0].astype(F32) + gwb[1].astype(F32)) + (gwb[2].astype(F32) + gwb[3].astype(F32))
    gk_ref[:, HALF:] = last_right.finish()

    for r in gi_copies:
        r.wait()
    for e in gi_own + q_out:
        e.wait()
    for r in li_copies + [w_copy] + gx + gf + g1:
        r.wait_send()
    last_left.drain()
    last_right.drain()
    for to_self, dev, src, dst, ssem, rsem in owners():

        @pl.when(jnp.logical_not(to_self))
        def _():
            remote(src, dst, ssem, rsem, dev).wait_send()


def shards(layer_input, queries, key_rows, grad_out, w_value, destination, seg_start):
    any_spec = pl.BlockSpec(memory_space=pl.ANY)
    vmem_spec = pl.BlockSpec(memory_space=pltpu.VMEM)
    dma = pltpu.SemaphoreType.DMA
    tokens = pltpu.VMEM
    return pl.pallas_call(
        kernel,
        out_shape=(
            jax.ShapeDtypeStruct(queries.shape, BF16),
            jax.ShapeDtypeStruct(key_rows.shape, BF16),
            jax.ShapeDtypeStruct(layer_input.shape, BF16),
            jax.ShapeDtypeStruct((64, KVW), F32),
        ),
        in_specs=[any_spec] * 5 + [vmem_spec] * 2,
        out_specs=(any_spec, vmem_spec, any_spec, vmem_spec),
        scratch_shapes=[
            tokens((RANKS, ROWS + SLOTS, KVW), BF16),
            tokens((RANKS, ROWS, KVW), BF16),
            tokens((RANKS, KVH, ROWS, HD), BF16),
            tokens((RANKS, KVH, ROWS, HD), BF16),
            tokens((RANKS, 10, SLOTS, KVW), BF16),
            tokens((RANKS, 10, SLOTS, KVW), BF16),
            tokens((RANKS, KVH, KEYS, ROWS), BF16),
            tokens((2, 8, ROWS, HALF), BF16),
            tokens((2, HALF, KVW), BF16),
            tokens((8, ROWS, KVW), BF16),
            tokens((4, ROWS, KVW), BF16),
            tokens((3, ROWS, KVW), BF16),
            tokens((8, ROWS, KVW), BF16),
            tokens((7, ROWS, KVW), BF16),
            tokens((8, ROWS, KVW), BF16),
            tokens((7, ROWS, KVW), BF16),
            tokens((8, ROWS, KVW), BF16),
            tokens((4, 4, 64, HALF), BF16),
            tokens((4, 4, 64, HALF), BF16),
            tokens((3, 4, 64, HALF), BF16),
            tokens((3, 4, 64, HALF), BF16),
            tokens((4, 64, HALF), BF16),
            tokens((4, 64, HALF), BF16),
            tokens((8, 256, 256), BF16),
            tokens((2, 256, 1024), BF16),
            tokens((RANKS, 10, SLOTS, ROWS), BF16),
            tokens((2, 256, ROWS), F32),
            tokens((RANKS, SLOTS, ROWS), F32),
            tokens((RANKS, SLOTS, ROWS), F32),
            dma((22,)),
            dma((2, 8)),
            dma((2, 8)),
            dma((2, 8)),
            dma((2, 8)),
            dma((2, 14)),
            dma((2,)),
            dma((2,)),
            dma((2, 3)),
            dma((4, 8)),
            dma((4, 8)),
            dma((4, 8)),
            dma((4, 8)),
            dma((2, 3)),
            dma((2, 4)),
            dma((2, 14)),
            dma((2, 6)),
            dma((8,)),
            dma((8,)),
            dma((8,)),
        ],
        name="packed_backward",
        compiler_params=pltpu.CompilerParams(
            collective_id=0, has_side_effects=True, vmem_limit_bytes=64 * 1024 * 1024
        ),
    )(
        layer_input, queries, key_rows, grad_out, w_value,
        destination.reshape(1, ROWS), seg_start.reshape(1, ROWS),
    )


def solution(mesh):
    both = P(("dp", "fsdp"), None)
    return jax.shard_map(
        shards,
        mesh=mesh,
        in_specs=(both, both, both, both, P("fsdp", None), P(("dp", "fsdp")), P(("dp", "fsdp"))),
        out_specs=(both, both, both, both),
        check_vma=False,
    )
```

```python
import functools

import jax
import jax.numpy as jnp
from jax import lax
from jax.experimental import pallas as pl
from jax.experimental.pallas import tpu as pltpu
from jax.sharding import PartitionSpec as P

MESH = pl.DeviceIdType.MESH
F32 = jnp.float32
BF16 = jnp.bfloat16
HD = 128
ROWS = 128
RANKS = 16
SLOTS = 16
KVH = 8
GROUP = 8
KVW = KVH * HD
HALF = 512
KEYS = 160
INV_ROOT = 1.0 / HD**0.5
LOG2E = 1.4426950408889634
LINE_STEPS = ((1, 0), (3, 0), (1, 1), (3, 1), (2, 0), (2, 1), (0, 1))


def dot(a, b):
    return jnp.dot(a, b, preferred_element_type=F32)


def dot_nt(a, b):
    return lax.dot_general(a, b, (((1,), (1,)), ((), ())), preferred_element_type=F32)


def dot_tn(a, b):
    return lax.dot_general(a, b, (((0,), (0,)), ((), ())), preferred_element_type=F32)


def device(y, zl, c, zh, x):
    return (y * 4 + zl * 2 + c, zh * 4 + x)


def kernel(
    li_ref, q_ref, k_ref, go_ref, w_ref, dest_ref, seg_ref,
    gq_ref, gk_ref, gi_ref, gw_ref,
    ka, va, qs, gos, xa, xb, probs, li, wm, vp, vsib, vrow, sb1, rb1, sb2, rb2, gva,
    ga, gb, ra, rbb, gwa, gwb, sel, selo, labk, labo, posl, startl,
    loc_sem, k_sem, kf_sem, v_sem, vf_sem, li_sem, w_sem, vs_sem, vx_sem,
    s1_sem, r1_sem, s2_sem, r2_sem, gx_sem, gf_sem, gi_sem, g1_sem, g2s_sem, g2r_sem, out_sem,
):
    d, f = lax.axis_index("dp"), lax.axis_index("fsdp")
    y, zl, c = d // 4, lax.rem(d // 2, 2), lax.rem(d, 2)
    zh, x = f // 4, lax.rem(f, 4)
    z = zh * 2 + zl
    sib = device(y, zl, 1 - c, zh, x)
    y_up, y_down, y_far = lax.rem(y + 1, 4), lax.rem(y + 3, 4), lax.rem(y + 2, 4)
    dev_up, dev_down = device(y_up, zl, c, zh, x), device(y_down, zl, c, zh, x)
    dev_z = device(y, 1 - zl, c, zh, x)

    def line_at(step, sign=1):
        return lax.rem(x + sign * step[0] + 4, 4), lax.rem(c + step[1], 2)

    def line_dev(step, sign=1):
        tx, tc = line_at(step, sign)
        return device(y, zl, tc, zh, tx)

    def remote(src, dst, ssem, rsem, dev):
        return pltpu.make_async_remote_copy(
            src_ref=src, dst_ref=dst, send_sem=ssem, recv_sem=rsem, device_id=dev, device_id_type=MESH
        )

    own_k = pltpu.make_async_copy(k_ref, ka.at[d, pl.ds(0, ROWS)], loc_sem.at[0])
    own_k.start()

    def load(ref, g, sem):
        e = pltpu.make_async_copy(ref.at[:, pl.ds(g * 1024, 1024)], vp.at[g], sem)
        e.start()
        return e

    q_loads = [load(q_ref, g, loc_sem.at[1 + g]) for g in range(KVH)]
    me_line = c * 4 + x
    li_own = []
    for h in range(2):
        e = pltpu.make_async_copy(
            li_ref.at[:, pl.ds(pl.multiple_of(h * 4096 + x * 1024 + c * HALF, HALF), HALF)],
            li.at[h, me_line],
            loc_sem.at[17 + h],
        )
        e.start()
        li_own += [e]
    own_rows = w_ref.at[pl.ds(pl.multiple_of(c * HALF, HALF), HALF)]
    w_own = pltpu.make_async_copy(own_rows, wm.at[zh], loc_sem.at[19])
    w_own.start()

    barrier = pltpu.get_barrier_semaphore()

    def greet(dev):
        pl.semaphore_signal(barrier, inc=1, device_id=dev, device_id_type=MESH)

    w_dev = device(y, 1 - zl, c, 1 - zh, x)
    z_devs = [device(y, lax.rem(z + i, 2), c, lax.rem(z + i, 4) // 2, x) for i in (1, 2, 3)]
    y_devs = [device(lax.rem(y + i, 4), zl, c, zh, x) for i in (1, 2, 3)]
    x_src = lax.rem(y, 2) * 2 + zl
    in_own_line = x == x_src
    for dev in [dev_up, dev_down, dev_z, w_dev] + z_devs + y_devs:
        greet(dev)
    for step in LINE_STEPS:
        greet(line_dev(step, -1))
    y_src = 2 * (y // 2) + x // 2
    for i in range(4):

        @pl.when(jnp.logical_not(in_own_line & (y == i) & (zl == lax.rem(x, 2))))
        def _():
            greet(device(i, lax.rem(x, 2), c, zh, x_src))

        @pl.when(jnp.logical_not(in_own_line & (y == y_src) & (z == i)))
        def _():
            greet(device(y_src, i % 2, c, i // 2, x_src))

    pl.semaphore_wait(barrier, 10 + 7 + 8 - 2 * in_own_line.astype(jnp.int32))

    dest = jnp.broadcast_to(dest_ref[...], (SLOTS, ROWS))
    block = (dest >> 7).astype(F32)
    label = (dest & 127).astype(F32) + 1.0
    seg = jnp.broadcast_to(seg_ref[...], (SLOTS, ROWS)).astype(F32)
    ka[d, ROWS:, :] = jnp.concatenate(
        [block, label, seg] + [jnp.zeros((SLOTS, ROWS), F32)] * 5, axis=1
    ).astype(BF16)
    own_k.wait()

    class Gather:
        def __init__(self, buf, rows, sems, fsems, base=0, lanes=pl.ds(0, KVW)):
            chips = [(y, zl), (y, 1 - zl), (y_down, zl), (y_up, zl)]
            chips += [(y_down, 1 - zl), (y_up, 1 - zl), (y_far, zl), (y_far, 1 - zl)]
            self.q = [cy * 2 + cz for cy, cz in chips]
            me, zs, yd, yu, _, _, yo, _ = [q * 2 + c for q in self.q]

            def hop(i, slot, dev, first=0, count=rows):
                part = buf.at[slot, pl.ds(first, count), lanes]
                return remote(part, part, sems.at[base, i], sems.at[base + 1, i], dev)

            self.hops = [
                hop(0, me, dev_up), hop(1, me, dev_down), hop(2, me, dev_z),
                hop(3, zs, dev_up), hop(4, zs, dev_down),
                hop(5, yd, dev_up, 0, 64), hop(6, yu, dev_down, 64, rows - 64),
                hop(7, yo, dev_z),
            ]
            self.twin = [
                remote(
                    buf.at[q * 2 + c, pl.ds(0, rows), lanes], buf.at[q * 2 + c, pl.ds(0, rows), lanes],
                    fsems.at[base, j], fsems.at[base + 1, j], sib,
                )
                for j, q in enumerate(self.q)
            ]

        def start(self):
            for r in self.hops[:3] + self.twin[:1]:
                r.start()

        def second(self):
            hops, twin = self.hops, self.twin
            hops[2].wait_recv()
            for r in (hops[3], hops[4], twin[1]):
                r.start()
            hops[0].wait_recv()
            for r in (hops[5], twin[2]):
                r.start()
            hops[1].wait_recv()
            for r in (hops[6], twin[3]):
                r.start()

        def third(self):
            hops, twin = self.hops, self.twin
            hops[5].wait_recv()
            hops[6].wait_recv()
            for r in (hops[7], twin[6]):
                r.start()
            hops[3].wait_recv()
            twin[4].start()
            hops[4].wait_recv()
            twin[5].start()

        def fourth(self):
            self.hops[7].wait_recv()
            self.twin[7].start()

        def take(self, which, taker):
            for j in which:
                self.twin[j].wait_recv()
                taker(self.q[j])

        def drain(self):
            for r in self.hops + self.twin:
                r.wait_send()

    keys = [
        Gather(ka, ROWS + SLOTS * (1 - half), k_sem, kf_sem, half * 2, pl.ds(half * HALF, HALF))
        for half in range(2)
    ]
    keys[0].start()
    keys[1].start()
    li_copies = []
    for o, step in enumerate(LINE_STEPS):
        tx, tc = line_at(step)
        for h in range(2):
            r = remote(
                li_ref.at[:, pl.ds(pl.multiple_of(h * 4096 + tx * 1024 + tc * HALF, HALF), HALF)],
                li.at[h, me_line],
                li_sem.at[0, o * 2 + h],
                li_sem.at[1, o * 2 + h],
                line_dev(step),
            )
            r.start()
            li_copies += [r]
    w_copy = remote(own_rows, wm.at[zh], w_sem.at[0], w_sem.at[1], w_dev)
    w_copy.start()

    rows16 = lax.broadcasted_iota(jnp.int32, (SLOTS, ROWS), 0).astype(F32)
    tri = (
        lax.broadcasted_iota(jnp.int32, (ROWS, ROWS), 0)
        < lax.broadcasted_iota(jnp.int32, (ROWS, ROWS), 1)
    ).astype(F32).astype(BF16)
    ones = jnp.ones((ROWS, ROWS), BF16)
    rows256 = lax.broadcasted_iota(jnp.int32, (256, ROWS), 0).astype(F32)
    lane1 = lax.broadcasted_iota(jnp.int32, (ROWS, ROWS), 1).astype(F32) + 1.0
    low4 = (lax.broadcasted_iota(jnp.int32, (ROWS, ROWS), 0) & 15).astype(F32)

    def ranks_of(block16):
        hot = (block16 == rows16).astype(F32)
        return jnp.sum(hot * dot(hot.astype(BF16), tri), axis=0, keepdims=True)

    own_slot = block[0:1] * SLOTS + ranks_of(block)
    own_sel = (rows256 == own_slot).astype(F32).astype(BF16)

    def by_block(g, dst):
        placed = dot(own_sel, vp[g]).astype(BF16)
        for h in range(GROUP):
            dst[:, g, h * SLOTS : (h + 1) * SLOTS, :] = placed[:, h * HD : (h + 1) * HD].reshape(
                RANKS, SLOTS, HD
            )

    go_loads = []
    for g in range(KVH):
        q_loads[g].wait()
        by_block(g, qs)
        go_loads += [load(go_ref, g, loc_sem.at[9 + g])]
    keys[0].second()
    for g in range(KVH):
        go_loads[g].wait()
        by_block(g, gos)
    keys[1].second()
    keys[0].third()

    def take_keys(q):
        for core in range(2):
            s = q * 2 + core
            extra = ka[s, ROWS:, 0:384].astype(F32)
            block_s, label_s, seg_s = extra[:, 0:128], extra[:, 128:256], extra[:, 256:384]
            rank = ranks_of(block_s)
            base = block_s[0:1] * SLOTS
            main = jnp.where(rank < 8.0, base + core * 8 + rank, -1.0)
            slot8 = (lax.rem(s, 8) * 2).astype(F32)
            over = jnp.where(rank < 8.0, -1.0, base + slot8 + rank - 8.0)
            hot = (rows256 == main).astype(F32)
            sel[q, :, core * ROWS : (core + 1) * ROWS] = hot.astype(BF16)
            hot_over = (rows256 == over).astype(F32)
            lanes = pl.ds(pl.multiple_of(lax.rem(s, 8) * ROWS, ROWS), ROWS)
            selo[s // 8, :, lanes] = hot_over.astype(BF16)
            marks = dot((hot * label_s[0:1]).astype(BF16), ones)
            marks = marks if core == 0 else marks + before
            before = marks
            labo[s // 8] += dot((hot_over * label_s[0:1]).astype(BF16), ones)
            mine = (low4 + (s * SLOTS).astype(F32) == own_slot).astype(F32)
            columns = dot((mine * label[0:1]).astype(BF16), ones)
            at_row = (columns == lane1).astype(F32).astype(BF16)
            posl[s] = dot_nt(label.astype(BF16), mine.astype(BF16))
            startl[s] = dot_nt(seg_s.astype(BF16), at_row) + 1.0
        labk[:, q] = marks.astype(BF16).reshape(RANKS, SLOTS, ROWS)
        take_pair(ka, xa, q, slice(0, HALF))

    def take_pair(buf, dst, q, cols=slice(0, KVW)):
        pair = buf[pl.ds(q * 2, 2), 0:ROWS, cols].reshape(2 * ROWS, -1)
        dst[:, q, :, cols] = dot(sel[q], pair).astype(BF16).reshape(RANKS, SLOTS, -1)

    def take_over(buf, dst, cols=slice(0, KVW)):
        for part in range(2):
            rows = buf[part * 8 : part * 8 + 8, 0:ROWS, cols].reshape(8 * ROWS, -1)
            dst[:, 8 + part, :, cols] = dot(selo[part], rows).astype(BF16).reshape(RANKS, SLOTS, -1)

    labo[...] = jnp.zeros_like(labo)
    keys[0].take((0, 1, 2, 3), take_keys)
    keys[0].fourth()
    keys[1].third()
    keys[0].take((4, 5, 6, 7), take_keys)
    take_over(ka, xa, slice(0, HALF))
    for half in range(2):
        labk[:, 8 + half] = labo[half].astype(BF16).reshape(RANKS, SLOTS, ROWS)

    def first_pass(half, first, last):
        def block_step(t, _):
            marks = labk[t].reshape(KEYS, ROWS).astype(F32)
            bias = jnp.where((marks <= posl[t][0:1]) & (marks >= startl[t][0:1]), 0.0, -1e30)
            heads = range(half * 4, half * 4 + 4)
            cols = [slice(g * HD, (g + 1) * HD) for g in heads]
            scores = [dot_nt(xa[t, :, :, at].reshape(KEYS, HD), qs[t, g]) for g, at in zip(heads, cols)]
            scores = [v * (INV_ROOT * LOG2E) + bias for v in scores]
            peaks = [jnp.maximum(jnp.max(v, axis=0, keepdims=True), -1e29) for v in scores]
            expos = [jnp.exp2(v - peak) for v, peak in zip(scores, peaks)]
            totals = [jnp.maximum(jnp.sum(v, axis=0, keepdims=True), 0.5) for v in expos]
            lows = [(v * (1.0 / total)).astype(BF16) for v, total in zip(expos, totals)]
            parts = [dot(low, gos[t, g]).astype(BF16) for g, low in zip(heads, lows)]
            for g, at, low, part in zip(heads, cols, lows, parts):
                probs[t, g] = low
                xb[t, :, :, at] = part.reshape(10, SLOTS, HD)
            return 0

        lax.fori_loop(first, last, block_step, 0)

    keys[1].fourth()
    first_pass(0, 0, 16)

    for e in li_own:
        e.wait()
    w_own.wait()
    for r in li_copies:
        r.wait_recv()
    w_copy.wait_recv()

    def value_term(core):
        def chunk(n, _):
            cols = pl.ds(pl.multiple_of(n * 256, 256), 256)
            part = dot(li[0, pl.ds(core * 4, 4)].reshape(HALF, HALF), wm[0, :, cols])
            part += dot(li[1, pl.ds(core * 4, 4)].reshape(HALF, HALF), wm[1, :, cols])
            vp[pl.ds(core * 4, 4), :, cols] = part.astype(BF16).reshape(4, ROWS, 256)
            return 0

        lax.fori_loop(0, 4, chunk, 0)

    value_term(1 - c)
    v_sib = remote(vp.at[pl.ds((1 - c) * 4, 4)], vsib, vs_sem.at[0], vs_sem.at[1], sib)
    v_sib.start()
    value_term(c)
    right_cols = slice(HALF, KVW)
    keys[1].take(range(8), lambda q: take_pair(ka, xa, q, right_cols))
    take_over(ka, xa, right_cols)

    v_sib.wait_recv()
    vx = []
    own_v = None
    for o, dx in enumerate((2, 1, 3)):
        tx = lax.rem(x + dx, 4)
        vp[c * 4 + tx] = (vp[c * 4 + tx].astype(F32) + vsib[tx].astype(F32)).astype(BF16)
        r = remote(
            vp.at[c * 4 + tx], vrow.at[o], vx_sem.at[0, o], vx_sem.at[1, o],
            device(y, zl, c, zh, tx),
        )
        r.start()
        vx += [r]
    keys[0].drain()
    keys[1].drain()

    class Scatter:
        def __init__(self, half, sb, rb, ssems, rsems):
            self.sb, self.rb = sb, rb
            self.cols = slice(half * HALF, (half + 1) * HALF)
            lanes = pl.ds(half * HALF, HALF)
            base = half * 2
            self.twin = [
                remote(
                    ka.at[(1 - c) * 8 + q, pl.ds(0, ROWS), lanes], sb.at[q, :, lanes],
                    ssems.at[base, q], ssems.at[base + 1, q], sib,
                )
                for q in range(8)
            ]
            oz = 1 - zl
            plan = (
                (y_far * 2 + oz, 0, 0, ROWS, dev_z), (y_up * 2 + oz, 1, 0, ROWS, dev_up),
                (y_down * 2 + oz, 2, 0, ROWS, dev_down),
                (y_far * 2 + zl, 3, 0, 64, dev_up), (y_far * 2 + zl, 3, 64, 64, dev_down),
                (y * 2 + oz, 4, 0, ROWS, dev_z),
                (y_up * 2 + zl, 5, 0, ROWS, dev_up), (y_down * 2 + zl, 6, 0, ROWS, dev_down),
            )
            self.hops = [
                remote(
                    ka.at[c * 8 + q, pl.ds(first, count), lanes],
                    rb.at[slot, pl.ds(first, count), lanes],
                    rsems.at[base, i], rsems.at[base + 1, i], dev,
                )
                for i, (q, slot, first, count, dev) in enumerate(plan)
            ]

        def part(self, q, core):
            s = q * 2 + core
            lanes = pl.ds(pl.multiple_of(core * ROWS, ROWS), ROWS)
            total = dot_tn(sel[q, :, lanes], xb[:, q, :, self.cols].reshape(256, HALF))
            lanes = pl.ds(pl.multiple_of(lax.rem(s, 8) * ROWS, ROWS), ROWS)
            rows = xb[:, 8 + s // 8, :, self.cols].reshape(256, HALF)
            return total + dot_tn(selo[s // 8, :, lanes], rows)

        def start(self):
            for q in range(8):
                ka[(1 - c) * 8 + q, 0:ROWS, self.cols] = self.part(q, 1 - c).astype(BF16)
                self.twin[q].start()

        def join(self, q):
            total = self.part(q, c) + self.sb[q, :, self.cols].astype(F32)
            ka[c * 8 + q, 0:ROWS, self.cols] = total.astype(BF16)

        def first(self):
            for r in self.twin:
                r.wait_recv()
            oz = 1 - zl
            for i, q in enumerate((y_far * 2 + oz, y_up * 2 + oz, y_down * 2 + oz)):
                self.join(q)
                self.hops[i].start()
            for q in (y_far * 2 + zl, y * 2 + oz, y_up * 2 + zl, y_down * 2 + zl, y * 2 + zl):
                self.join(q)

        def add(self, q, slots, first=0, count=ROWS):
            at = (c * 8 + q, slice(first, first + count), self.cols)
            total = ka[at].astype(F32)
            for slot in slots:
                total = total + self.rb[slot, first : first + count, self.cols].astype(F32)
            ka[at] = total.astype(BF16)

        def second(self):
            self.hops[0].wait_recv()
            self.add(y_far * 2 + zl, (0,))
            self.hops[3].start()
            self.hops[4].start()
            self.hops[1].wait_recv()
            self.hops[2].wait_recv()
            self.add(y * 2 + 1 - zl, (1, 2))
            self.hops[5].start()

        def third(self):
            self.hops[3].wait_recv()
            self.add(y_up * 2 + zl, (3,), 0, 64)
            self.hops[6].start()
            self.hops[4].wait_recv()
            self.add(y_down * 2 + zl, (3,), 64, 64)
            self.hops[7].start()

        def finish(self):
            for i in (5, 6, 7):
                self.hops[i].wait_recv()
            total = ka[c * 8 + y * 2 + zl, 0:ROWS, self.cols].astype(F32)
            for slot in (4, 5, 6):
                total = total + self.rb[slot, :, self.cols].astype(F32)
            return total.astype(BF16)

        def drain(self):
            for r in self.hops + self.twin:
                r.wait_send()

    left = Scatter(0, sb1, rb1, s1_sem, r1_sem)
    right = Scatter(1, sb1, rb1, s1_sem, r1_sem)
    left.start()
    first_pass(1, 0, 6)
    left.first()
    first_pass(1, 6, 12)
    left.second()
    vsum = vp[c * 4 + x].astype(F32) + vsib[x].astype(F32)
    for o in range(3):
        vx[o].wait_recv()
        vsum = vsum + vrow[o].astype(F32)
    va[d] = vsum.astype(BF16)
    vals = [
        Gather(va, ROWS, v_sem, vf_sem, half * 2, pl.ds(half * HALF, HALF)) for half in range(2)
    ]

    gx = [[], []]
    gf = [[], []]

    def grad_hop(half, slot, sems, i, dev):
        part = gva.at[slot, :, pl.ds(half * HALF, HALF)]
        r = remote(part, part, sems.at[half * 2, i], sems.at[half * 2 + 1, i], dev)
        r.start()
        return r

    def grads_out(half, total):
        gva[me_line, :, half * HALF : (half + 1) * HALF] = total
        for o, dx in enumerate((2, 1, 3)):
            gx[half] += [grad_hop(half, me_line, gx_sem, o, device(y, zl, c, zh, lax.rem(x + dx, 4)))]
        gf[half] += [grad_hop(half, me_line, gf_sem, 3, sib)]

    def grads_on(half):
        for o, dx in enumerate((2, 1, 3)):
            gx[half][o].wait_recv()
            gf[half] += [grad_hop(half, c * 4 + lax.rem(x - dx + 4, 4), gf_sem, o, sib)]

    def take_values(half):
        cols = slice(half * HALF, (half + 1) * HALF)
        vals[half].take(range(8), lambda q: take_pair(va, xb, q, cols))
        take_over(va, xb, cols)

    vals[0].start()
    first_pass(1, 12, 16)
    left.third()
    right.start()
    vals[0].second()
    vals[1].start()
    right.first()
    grads_out(0, left.finish())
    vals[0].third()
    right.second()
    vals[1].second()
    vals[0].fourth()
    right.third()
    vals[1].third()
    grads_out(1, right.finish())
    take_values(0)

    def second_pass(half, first, last):
        def block_step(t, _):
            heads = range(half * 4, half * 4 + 4)
            cols = [slice(g * HD, (g + 1) * HD) for g in heads]
            grad_probs = [dot_nt(xb[t, :, :, at].reshape(KEYS, HD), gos[t, g]) for g, at in zip(heads, cols)]
            lows = [probs[t, g].astype(F32) for g in heads]
            row_dots = [jnp.sum(low * v, axis=0, keepdims=True) for low, v in zip(lows, grad_probs)]
            grad_scores = [
                (low * (v - dots)).astype(BF16) for low, v, dots in zip(lows, grad_probs, row_dots)
            ]
            key_parts = [dot(v, qs[t, g]) * INV_ROOT for v, g in zip(grad_scores, heads)]
            query_parts = [
                dot_tn(v, xa[t, :, :, at].reshape(KEYS, HD)) * INV_ROOT
                for v, at in zip(grad_scores, cols)
            ]
            for g, at, key_part, query_part in zip(heads, cols, key_parts, query_parts):
                xb[t, :, :, at] = key_part.astype(BF16).reshape(10, SLOTS, HD)
                qs[t, g] = query_part.astype(BF16)
            return 0

        lax.fori_loop(first, last, block_step, 0)

    second_pass(0, 0, 8)
    vals[1].fourth()
    grads_on(0)
    second_pass(0, 8, 16)
    left.drain()
    right.drain()
    last_left = Scatter(0, sb2, rb2, s2_sem, r2_sem)
    last_right = Scatter(1, sb2, rb2, s2_sem, r2_sem)
    last_left.start()
    grads_on(1)
    take_values(1)
    last_left.first()
    for r in vx + [v_sib]:
        r.wait_send()
    for r in gf[0] + gf[1]:
        r.wait_recv()

    def input_term(n, _):
        h, first = n // 2, pl.multiple_of(lax.rem(n, 2) * 256, 256)
        part = dot_nt(gva[...].reshape(1024, KVW), wm[h, pl.ds(first, 256), :])
        cols = pl.ds(pl.multiple_of(n * 256, 256), 256)
        vp[:, :, cols] = part.astype(BF16).reshape(8, ROWS, 256)
        return 0

    gi_copies = []
    gi_own = []
    for h in range(2):
        lax.fori_loop(h * 2, h * 2 + 2, input_term, 0)
        gi_cols = pl.ds(pl.multiple_of(h * 4096 + x * 1024 + c * HALF, HALF), HALF)
        for o, step in enumerate(LINE_STEPS):
            tx, tc = line_at(step)
            r = remote(
                vp.at[tc * 4 + tx, :, pl.ds(h * HALF, HALF)], gi_ref.at[:, gi_cols],
                gi_sem.at[0, o * 2 + h], gi_sem.at[1, o * 2 + h], line_dev(step),
            )
            r.start()
            gi_copies += [r]
        e = pltpu.make_async_copy(
            vp.at[me_line, :, pl.ds(h * HALF, HALF)], gi_ref.at[:, gi_cols], loc_sem.at[20 + h]
        )
        e.start()
        gi_own += [e]

    for h in range(2):
        for n in range(4):
            part = dot_tn(
                li[h].reshape(1024, HALF), gva[:, :, n * 256 : (n + 1) * 256].reshape(1024, 256)
            )
            part = part.astype(BF16).reshape(8, 64, 256)
            cols = slice((n % 2) * 256, (n % 2) * 256 + 256)
            for fb in range(8):
                zt, x1, x0 = fb // 4, (fb // 2) % 2, fb % 2
                if n < 2:
                    ga[zt * 2 + x0, h * 2 + x1, :, cols] = part[fb]
                else:
                    gb[h * 2 + x1, zt * 2 + x0, :, cols] = part[fb]
    g1 = []
    for i in range(3):
        r = remote(ga.at[lax.rem(z + i + 1, 4)], ra.at[i], g1_sem.at[0, i], g1_sem.at[1, i], z_devs[i])
        r.start()
        g1 += [r]
        r = remote(
            gb.at[lax.rem(y + i + 1, 4)], rbb.at[i], g1_sem.at[0, 3 + i], g1_sem.at[1, 3 + i], y_devs[i]
        )
        r.start()
        g1 += [r]

    last_left.second()
    second_pass(1, 0, 8)
    last_left.third()
    second_pass(1, 8, 16)
    last_right.start()
    for v in vals:
        v.drain()

    q_out = []

    def queries_out(g):
        slots = jnp.concatenate(
            [qs[:, g, h * SLOTS : (h + 1) * SLOTS, :].reshape(256, HD) for h in range(GROUP)], axis=1
        )
        va[g] = dot_tn(own_sel, slots).astype(BF16)
        e = pltpu.make_async_copy(va.at[g], gq_ref.at[:, pl.ds(g * 1024, 1024)], out_sem.at[g])
        e.start()
        q_out.append(e)

    for g in range(4):
        queries_out(g)
    last_right.first()
    gk_ref[:, 0:HALF] = last_left.finish()
    for r in g1:
        r.wait_recv()
    ga[z] = (
        ga[z].astype(F32) + ra[0].astype(F32) + ra[1].astype(F32) + ra[2].astype(F32)
    ).astype(BF16)
    gb[y] = (
        gb[y].astype(F32) + rbb[0].astype(F32) + rbb[1].astype(F32) + rbb[2].astype(F32)
    ).astype(BF16)

    def owners():
        for i in range(4):
            h, x1 = i // 2, i % 2
            ty, tx = 2 * h + x // 2, x1 * 2 + zl
            yield (
                in_own_line & (ty == y) & (tx == x), device(ty, lax.rem(x, 2), c, zh, tx),
                ga.at[z, i], gwa.at[y], g2s_sem.at[i], g2r_sem.at[y],
            )
            zt, x0 = i // 2, i % 2
            ty, tx = 2 * (y // 2) + x // 2, lax.rem(y, 2) * 2 + x0
            yield (
                in_own_line & (zt == zh) & (tx == x), device(ty, lax.rem(x, 2), c, zt, tx),
                gb.at[y, i], gwb.at[z], g2s_sem.at[4 + i], g2r_sem.at[4 + z],
            )

    for to_self, dev, src, dst, ssem, rsem in owners():

        @pl.when(to_self)
        def _():
            pltpu.make_async_copy(src, dst, rsem).start()

        @pl.when(jnp.logical_not(to_self))
        def _():
            remote(src, dst, ssem, rsem, dev).start()

    for g in range(4, KVH):
        queries_out(g)
    last_right.second()
    last_right.third()
    for i in range(4):
        pltpu.make_async_copy(gwa.at[i], gwa.at[i], g2r_sem.at[i]).wait()
        pltpu.make_async_copy(gwb.at[i], gwb.at[i], g2r_sem.at[4 + i]).wait()
    gw_ref[:, 0:HALF] = (gwa[0].astype(F32) + gwa[1].astype(F32)) + (gwa[2].astype(F32) + gwa[3].astype(F32))
    gw_ref[:, HALF:] = (gwb[0].astype(F32) + gwb[1].astype(F32)) + (gwb[2].astype(F32) + gwb[3].astype(F32))
    gk_ref[:, HALF:] = last_right.finish()

    for r in gi_copies:
        r.wait()
    for e in gi_own + q_out:
        e.wait()
    for r in li_copies + [w_copy] + gx[0] + gx[1] + gf[0] + gf[1] + g1:
        r.wait_send()
    last_left.drain()
    last_right.drain()
    for to_self, dev, src, dst, ssem, rsem in owners():

        @pl.when(jnp.logical_not(to_self))
        def _():
            remote(src, dst, ssem, rsem, dev).wait_send()


def shards(layer_input, queries, key_rows, grad_out, w_value, destination, seg_start):
    any_spec = pl.BlockSpec(memory_space=pl.ANY)
    vmem_spec = pl.BlockSpec(memory_space=pltpu.VMEM)
    dma = pltpu.SemaphoreType.DMA
    tokens = pltpu.VMEM
    return pl.pallas_call(
        kernel,
        out_shape=(
            jax.ShapeDtypeStruct(queries.shape, BF16),
            jax.ShapeDtypeStruct(key_rows.shape, BF16),
            jax.ShapeDtypeStruct(layer_input.shape, BF16),
            jax.ShapeDtypeStruct((64, KVW), F32),
        ),
        in_specs=[any_spec] * 5 + [vmem_spec] * 2,
        out_specs=(any_spec, vmem_spec, any_spec, vmem_spec),
        scratch_shapes=[
            tokens((RANKS, ROWS + SLOTS, KVW), BF16),
            tokens((RANKS, ROWS, KVW), BF16),
            tokens((RANKS, KVH, ROWS, HD), BF16),
            tokens((RANKS, KVH, ROWS, HD), BF16),
            tokens((RANKS, 10, SLOTS, KVW), BF16),
            tokens((RANKS, 10, SLOTS, KVW), BF16),
            tokens((RANKS, KVH, KEYS, ROWS), BF16),
            tokens((2, 8, ROWS, HALF), BF16),
            tokens((2, HALF, KVW), BF16),
            tokens((8, ROWS, KVW), BF16),
            tokens((4, ROWS, KVW), BF16),
            tokens((3, ROWS, KVW), BF16),
            tokens((8, ROWS, KVW), BF16),
            tokens((7, ROWS, KVW), BF16),
            tokens((8, ROWS, KVW), BF16),
            tokens((7, ROWS, KVW), BF16),
            tokens((8, ROWS, KVW), BF16),
            tokens((4, 4, 64, HALF), BF16),
            tokens((4, 4, 64, HALF), BF16),
            tokens((3, 4, 64, HALF), BF16),
            tokens((3, 4, 64, HALF), BF16),
            tokens((4, 64, HALF), BF16),
            tokens((4, 64, HALF), BF16),
            tokens((8, 256, 256), BF16),
            tokens((2, 256, 1024), BF16),
            tokens((RANKS, 10, SLOTS, ROWS), BF16),
            tokens((2, 256, ROWS), F32),
            tokens((RANKS, SLOTS, ROWS), F32),
            tokens((RANKS, SLOTS, ROWS), F32),
            dma((22,)),
            dma((4, 8)),
            dma((4, 8)),
            dma((4, 8)),
            dma((4, 8)),
            dma((2, 14)),
            dma((2,)),
            dma((2,)),
            dma((2, 3)),
            dma((4, 8)),
            dma((4, 8)),
            dma((4, 8)),
            dma((4, 8)),
            dma((4, 3)),
            dma((4, 4)),
            dma((2, 14)),
            dma((2, 6)),
            dma((8,)),
            dma((8,)),
            dma((8,)),
        ],
        name="packed_backward",
        compiler_params=pltpu.CompilerParams(
            collective_id=0, has_side_effects=True, vmem_limit_bytes=64 * 1024 * 1024
        ),
    )(
        layer_input, queries, key_rows, grad_out, w_value,
        destination.reshape(1, ROWS), seg_start.reshape(1, ROWS),
    )


def solution(mesh):
    both = P(("dp", "fsdp"), None)
    return jax.shard_map(
        shards,
        mesh=mesh,
        in_specs=(both, both, both, both, P("fsdp", None), P(("dp", "fsdp")), P(("dp", "fsdp"))),
        out_specs=(both, both, both, both),
        check_vma=False,
    )
```

```python
import functools

import jax
import jax.numpy as jnp
from jax import lax
from jax.experimental import pallas as pl
from jax.experimental.pallas import tpu as pltpu
from jax.sharding import PartitionSpec as P

MESH = pl.DeviceIdType.MESH
F32 = jnp.float32
BF16 = jnp.bfloat16
HD = 128
ROWS = 128
RANKS = 16
SLOTS = 16
KVH = 8
GROUP = 8
KVW = KVH * HD
HALF = 512
KEYS = 160
INV_ROOT = 1.0 / HD**0.5
LOG2E = 1.4426950408889634
LINE_STEPS = ((1, 0), (3, 0), (1, 1), (3, 1), (2, 0), (2, 1), (0, 1))


def dot(a, b):
    return jnp.dot(a, b, preferred_element_type=F32)


def dot_nt(a, b):
    return lax.dot_general(a, b, (((1,), (1,)), ((), ())), preferred_element_type=F32)


def dot_tn(a, b):
    return lax.dot_general(a, b, (((0,), (0,)), ((), ())), preferred_element_type=F32)


def device(y, zl, c, zh, x):
    return (y * 4 + zl * 2 + c, zh * 4 + x)


def kernel(
    li_ref, q_ref, k_ref, go_ref, w_ref, dest_ref, seg_ref,
    gq_ref, gk_ref, gi_ref, gw_ref,
    ka, va, qs, gos, xa, xb, probs, li, wm, vp, vsib, vrow, sb1, rb1, sb2, rb2, gva,
    ga, gb, ra, rbb, gwa, gwb, sel, selo, labk, labo, posl, startl,
    loc_sem, k_sem, kf_sem, v_sem, vf_sem, li_sem, w_sem, vs_sem, vx_sem,
    s1_sem, r1_sem, s2_sem, r2_sem, gx_sem, gf_sem, gi_sem, g1_sem, g2s_sem, g2r_sem, out_sem,
):
    d, f = lax.axis_index("dp"), lax.axis_index("fsdp")
    y, zl, c = d // 4, lax.rem(d // 2, 2), lax.rem(d, 2)
    zh, x = f // 4, lax.rem(f, 4)
    z = zh * 2 + zl
    sib = device(y, zl, 1 - c, zh, x)
    y_up, y_down, y_far = lax.rem(y + 1, 4), lax.rem(y + 3, 4), lax.rem(y + 2, 4)
    dev_up, dev_down = device(y_up, zl, c, zh, x), device(y_down, zl, c, zh, x)
    dev_z = device(y, 1 - zl, c, zh, x)

    def line_at(step, sign=1):
        return lax.rem(x + sign * step[0] + 4, 4), lax.rem(c + step[1], 2)

    def line_dev(step, sign=1):
        tx, tc = line_at(step, sign)
        return device(y, zl, tc, zh, tx)

    def remote(src, dst, ssem, rsem, dev):
        return pltpu.make_async_remote_copy(
            src_ref=src, dst_ref=dst, send_sem=ssem, recv_sem=rsem, device_id=dev, device_id_type=MESH
        )

    own_k = pltpu.make_async_copy(k_ref, ka.at[d, pl.ds(0, ROWS)], loc_sem.at[0])
    own_k.start()

    def load(ref, g, sem):
        e = pltpu.make_async_copy(ref.at[:, pl.ds(g * 1024, 1024)], vp.at[g], sem)
        e.start()
        return e

    q_loads = [load(q_ref, g, loc_sem.at[1 + g]) for g in range(KVH)]
    me_line = c * 4 + x
    li_own = []
    for h in range(2):
        e = pltpu.make_async_copy(
            li_ref.at[:, pl.ds(pl.multiple_of(h * 4096 + x * 1024 + c * HALF, HALF), HALF)],
            li.at[h, me_line],
            loc_sem.at[17 + h],
        )
        e.start()
        li_own += [e]
    own_rows = w_ref.at[pl.ds(pl.multiple_of(c * HALF, HALF), HALF)]
    w_own = pltpu.make_async_copy(own_rows, wm.at[zh], loc_sem.at[19])
    w_own.start()

    barrier = pltpu.get_barrier_semaphore()

    def greet(dev):
        pl.semaphore_signal(barrier, inc=1, device_id=dev, device_id_type=MESH)

    w_dev = device(y, 1 - zl, c, 1 - zh, x)
    z_devs = [device(y, lax.rem(z + i, 2), c, lax.rem(z + i, 4) // 2, x) for i in (1, 2, 3)]
    y_devs = [device(lax.rem(y + i, 4), zl, c, zh, x) for i in (1, 2, 3)]
    x_src = lax.rem(y, 2) * 2 + zl
    in_own_line = x == x_src
    for dev in [dev_up, dev_down, dev_z, w_dev] + z_devs + y_devs:
        greet(dev)
    for step in LINE_STEPS:
        greet(line_dev(step, -1))
    y_src = 2 * (y // 2) + x // 2
    for i in range(4):

        @pl.when(jnp.logical_not(in_own_line & (y == i) & (zl == lax.rem(x, 2))))
        def _():
            greet(device(i, lax.rem(x, 2), c, zh, x_src))

        @pl.when(jnp.logical_not(in_own_line & (y == y_src) & (z == i)))
        def _():
            greet(device(y_src, i % 2, c, i // 2, x_src))

    pl.semaphore_wait(barrier, 10 + 7 + 8 - 2 * in_own_line.astype(jnp.int32))

    dest = jnp.broadcast_to(dest_ref[...], (SLOTS, ROWS))
    block = (dest >> 7).astype(F32)
    label = (dest & 127).astype(F32) + 1.0
    seg = jnp.broadcast_to(seg_ref[...], (SLOTS, ROWS)).astype(F32)
    ka[d, ROWS:, :] = jnp.concatenate(
        [block, label, seg] + [jnp.zeros((SLOTS, ROWS), F32)] * 5, axis=1
    ).astype(BF16)
    own_k.wait()

    class Gather:
        def __init__(self, buf, rows, sems, fsems, base=0, lanes=pl.ds(0, KVW)):
            chips = [(y, zl), (y, 1 - zl), (y_down, zl), (y_up, zl)]
            chips += [(y_down, 1 - zl), (y_up, 1 - zl), (y_far, zl), (y_far, 1 - zl)]
            self.q = [cy * 2 + cz for cy, cz in chips]
            me, zs, yd, yu, _, _, yo, _ = [q * 2 + c for q in self.q]

            def hop(i, slot, dev, first=0, count=rows):
                part = buf.at[slot, pl.ds(first, count), lanes]
                return remote(part, part, sems.at[base, i], sems.at[base + 1, i], dev)

            self.hops = [
                hop(0, me, dev_up), hop(1, me, dev_down), hop(2, me, dev_z),
                hop(3, zs, dev_up), hop(4, zs, dev_down),
                hop(5, yd, dev_up, 0, 64), hop(6, yu, dev_down, 64, rows - 64),
                hop(7, yo, dev_z),
            ]
            self.twin = [
                remote(
                    buf.at[q * 2 + c, pl.ds(0, rows), lanes], buf.at[q * 2 + c, pl.ds(0, rows), lanes],
                    fsems.at[base, j], fsems.at[base + 1, j], sib,
                )
                for j, q in enumerate(self.q)
            ]

        def start(self):
            for r in self.hops[:3] + self.twin[:1]:
                r.start()

        def second(self):
            hops, twin = self.hops, self.twin
            hops[2].wait_recv()
            for r in (hops[3], hops[4], twin[1]):
                r.start()
            hops[0].wait_recv()
            for r in (hops[5], twin[2]):
                r.start()
            hops[1].wait_recv()
            for r in (hops[6], twin[3]):
                r.start()

        def third(self):
            hops, twin = self.hops, self.twin
            hops[5].wait_recv()
            hops[6].wait_recv()
            for r in (hops[7], twin[6]):
                r.start()
            hops[3].wait_recv()
            twin[4].start()
            hops[4].wait_recv()
            twin[5].start()

        def fourth(self):
            self.hops[7].wait_recv()
            self.twin[7].start()

        def take(self, which, taker):
            for j in which:
                self.twin[j].wait_recv()
                taker(self.q[j])

        def drain(self):
            for r in self.hops + self.twin:
                r.wait_send()

    keys = [
        Gather(ka, ROWS + SLOTS * (1 - half), k_sem, kf_sem, half * 2, pl.ds(half * HALF, HALF))
        for half in range(2)
    ]
    keys[0].start()
    keys[1].start()
    li_copies = []
    for o, step in enumerate(LINE_STEPS):
        tx, tc = line_at(step)
        for h in range(2):
            r = remote(
                li_ref.at[:, pl.ds(pl.multiple_of(h * 4096 + tx * 1024 + tc * HALF, HALF), HALF)],
                li.at[h, me_line],
                li_sem.at[0, o * 2 + h],
                li_sem.at[1, o * 2 + h],
                line_dev(step),
            )
            r.start()
            li_copies += [r]
    w_copy = remote(own_rows, wm.at[zh], w_sem.at[0], w_sem.at[1], w_dev)
    w_copy.start()

    rows16 = lax.broadcasted_iota(jnp.int32, (SLOTS, ROWS), 0).astype(F32)
    tri = (
        lax.broadcasted_iota(jnp.int32, (ROWS, ROWS), 0)
        < lax.broadcasted_iota(jnp.int32, (ROWS, ROWS), 1)
    ).astype(F32).astype(BF16)
    ones = jnp.ones((ROWS, ROWS), BF16)
    rows256 = lax.broadcasted_iota(jnp.int32, (256, ROWS), 0).astype(F32)
    lane1 = lax.broadcasted_iota(jnp.int32, (ROWS, ROWS), 1).astype(F32) + 1.0
    low4 = (lax.broadcasted_iota(jnp.int32, (ROWS, ROWS), 0) & 15).astype(F32)

    def ranks_of(block16):
        hot = (block16 == rows16).astype(F32)
        return jnp.sum(hot * dot(hot.astype(BF16), tri), axis=0, keepdims=True)

    own_slot = block[0:1] * SLOTS + ranks_of(block)
    own_sel = (rows256 == own_slot).astype(F32).astype(BF16)

    def by_block(g, dst):
        placed = dot(own_sel, vp[g]).astype(BF16)
        for h in range(GROUP):
            dst[:, g, h * SLOTS : (h + 1) * SLOTS, :] = placed[:, h * HD : (h + 1) * HD].reshape(
                RANKS, SLOTS, HD
            )

    go_loads = []
    for g in range(KVH):
        q_loads[g].wait()
        by_block(g, qs)
        go_loads += [load(go_ref, g, loc_sem.at[9 + g])]
    keys[0].second()
    for g in range(KVH):
        go_loads[g].wait()
        by_block(g, gos)
    keys[1].second()
    keys[0].third()

    def take_keys(q):
        for core in range(2):
            s = q * 2 + core
            extra = ka[s, ROWS:, 0:384].astype(F32)
            block_s, label_s, seg_s = extra[:, 0:128], extra[:, 128:256], extra[:, 256:384]
            rank = ranks_of(block_s)
            base = block_s[0:1] * SLOTS
            main = jnp.where(rank < 8.0, base + core * 8 + rank, -1.0)
            slot8 = (lax.rem(s, 8) * 2).astype(F32)
            over = jnp.where(rank < 8.0, -1.0, base + slot8 + rank - 8.0)
            hot = (rows256 == main).astype(F32)
            sel[q, :, core * ROWS : (core + 1) * ROWS] = hot.astype(BF16)
            hot_over = (rows256 == over).astype(F32)
            lanes = pl.ds(pl.multiple_of(lax.rem(s, 8) * ROWS, ROWS), ROWS)
            selo[s // 8, :, lanes] = hot_over.astype(BF16)
            marks = dot((hot * label_s[0:1]).astype(BF16), ones)
            marks = marks if core == 0 else marks + before
            before = marks
            labo[s // 8] += dot((hot_over * label_s[0:1]).astype(BF16), ones)
            mine = (low4 + (s * SLOTS).astype(F32) == own_slot).astype(F32)
            columns = dot((mine * label[0:1]).astype(BF16), ones)
            at_row = (columns == lane1).astype(F32).astype(BF16)
            posl[s] = dot_nt(label.astype(BF16), mine.astype(BF16))
            startl[s] = dot_nt(seg_s.astype(BF16), at_row) + 1.0
        labk[:, q] = marks.astype(BF16).reshape(RANKS, SLOTS, ROWS)
        take_pair(ka, xa, q, slice(0, HALF))

    def take_pair(buf, dst, q, cols=slice(0, KVW)):
        pair = buf[pl.ds(q * 2, 2), 0:ROWS, cols].reshape(2 * ROWS, -1)
        dst[:, q, :, cols] = dot(sel[q], pair).astype(BF16).reshape(RANKS, SLOTS, -1)

    def take_over(buf, dst, cols=slice(0, KVW)):
        for part in range(2):
            rows = buf[part * 8 : part * 8 + 8, 0:ROWS, cols].reshape(8 * ROWS, -1)
            dst[:, 8 + part, :, cols] = dot(selo[part], rows).astype(BF16).reshape(RANKS, SLOTS, -1)

    labo[...] = jnp.zeros_like(labo)
    keys[0].take((0, 1, 2, 3), take_keys)
    keys[0].fourth()
    keys[1].third()
    keys[0].take((4, 5, 6, 7), take_keys)
    take_over(ka, xa, slice(0, HALF))
    for half in range(2):
        labk[:, 8 + half] = labo[half].astype(BF16).reshape(RANKS, SLOTS, ROWS)

    def first_pass(half, first, last):
        def block_step(t, _):
            marks = labk[t].reshape(KEYS, ROWS).astype(F32)
            bias = jnp.where((marks <= posl[t][0:1]) & (marks >= startl[t][0:1]), 0.0, -1e30)
            heads = range(half * 4, half * 4 + 4)
            cols = [slice(g * HD, (g + 1) * HD) for g in heads]
            scores = [dot_nt(xa[t, :, :, at].reshape(KEYS, HD), qs[t, g]) for g, at in zip(heads, cols)]
            scores = [v * (INV_ROOT * LOG2E) + bias for v in scores]
            peaks = [jnp.maximum(jnp.max(v, axis=0, keepdims=True), -1e29) for v in scores]
            expos = [jnp.exp2(v - peak) for v, peak in zip(scores, peaks)]
            totals = [jnp.maximum(jnp.sum(v, axis=0, keepdims=True), 0.5) for v in expos]
            lows = [(v * (1.0 / total)).astype(BF16) for v, total in zip(expos, totals)]
            parts = [dot(low, gos[t, g]).astype(BF16) for g, low in zip(heads, lows)]
            for g, at, low, part in zip(heads, cols, lows, parts):
                probs[t, g] = low
                xb[t, :, :, at] = part.reshape(10, SLOTS, HD)
            return 0

        lax.fori_loop(first, last, block_step, 0)

    keys[1].fourth()
    first_pass(0, 0, 16)

    for e in li_own:
        e.wait()
    w_own.wait()
    for r in li_copies:
        r.wait_recv()
    w_copy.wait_recv()

    def value_term(core):
        def chunk(n, _):
            cols = pl.ds(pl.multiple_of(n * 256, 256), 256)
            part = dot(li[0, pl.ds(core * 4, 4)].reshape(HALF, HALF), wm[0, :, cols])
            part += dot(li[1, pl.ds(core * 4, 4)].reshape(HALF, HALF), wm[1, :, cols])
            vp[pl.ds(core * 4, 4), :, cols] = part.astype(BF16).reshape(4, ROWS, 256)
            return 0

        lax.fori_loop(0, 4, chunk, 0)

    value_term(1 - c)
    v_sib = remote(vp.at[pl.ds((1 - c) * 4, 4)], vsib, vs_sem.at[0], vs_sem.at[1], sib)
    v_sib.start()
    value_term(c)
    right_cols = slice(HALF, KVW)
    keys[1].take(range(8), lambda q: take_pair(ka, xa, q, right_cols))
    take_over(ka, xa, right_cols)

    v_sib.wait_recv()
    vx = [[], []]
    for half in range(2):
        cols = slice(half * HALF, (half + 1) * HALF)
        for o, dx in enumerate((2, 1, 3)):
            tx = lax.rem(x + dx, 4)
            total = vp[c * 4 + tx, :, cols].astype(F32) + vsib[tx, :, cols].astype(F32)
            vp[c * 4 + tx, :, cols] = total.astype(BF16)
            lanes = pl.ds(half * HALF, HALF)
            r = remote(
                vp.at[c * 4 + tx, :, lanes], vrow.at[o, :, lanes],
                vx_sem.at[half * 2, o], vx_sem.at[half * 2 + 1, o], device(y, zl, c, zh, tx),
            )
            r.start()
            vx[half] += [r]
    keys[0].drain()
    keys[1].drain()

    class Scatter:
        def __init__(self, half, sb, rb, ssems, rsems):
            self.sb, self.rb = sb, rb
            self.cols = slice(half * HALF, (half + 1) * HALF)
            lanes = pl.ds(half * HALF, HALF)
            base = half * 2
            self.twin = [
                remote(
                    ka.at[(1 - c) * 8 + q, pl.ds(0, ROWS), lanes], sb.at[q, :, lanes],
                    ssems.at[base, q], ssems.at[base + 1, q], sib,
                )
                for q in range(8)
            ]
            oz = 1 - zl
            plan = (
                (y_far * 2 + oz, 0, 0, ROWS, dev_z), (y_up * 2 + oz, 1, 0, ROWS, dev_up),
                (y_down * 2 + oz, 2, 0, ROWS, dev_down),
                (y_far * 2 + zl, 3, 0, 64, dev_up), (y_far * 2 + zl, 3, 64, 64, dev_down),
                (y * 2 + oz, 4, 0, ROWS, dev_z),
                (y_up * 2 + zl, 5, 0, ROWS, dev_up), (y_down * 2 + zl, 6, 0, ROWS, dev_down),
            )
            self.hops = [
                remote(
                    ka.at[c * 8 + q, pl.ds(first, count), lanes],
                    rb.at[slot, pl.ds(first, count), lanes],
                    rsems.at[base, i], rsems.at[base + 1, i], dev,
                )
                for i, (q, slot, first, count, dev) in enumerate(plan)
            ]

        def part(self, q, core):
            s = q * 2 + core
            lanes = pl.ds(pl.multiple_of(core * ROWS, ROWS), ROWS)
            total = dot_tn(sel[q, :, lanes], xb[:, q, :, self.cols].reshape(256, HALF))
            lanes = pl.ds(pl.multiple_of(lax.rem(s, 8) * ROWS, ROWS), ROWS)
            rows = xb[:, 8 + s // 8, :, self.cols].reshape(256, HALF)
            return total + dot_tn(selo[s // 8, :, lanes], rows)

        def start(self):
            for q in range(8):
                ka[(1 - c) * 8 + q, 0:ROWS, self.cols] = self.part(q, 1 - c).astype(BF16)
                self.twin[q].start()

        def join(self, q):
            total = self.part(q, c) + self.sb[q, :, self.cols].astype(F32)
            ka[c * 8 + q, 0:ROWS, self.cols] = total.astype(BF16)

        def first(self):
            for r in self.twin:
                r.wait_recv()
            oz = 1 - zl
            for i, q in enumerate((y_far * 2 + oz, y_up * 2 + oz, y_down * 2 + oz)):
                self.join(q)
                self.hops[i].start()
            for q in (y_far * 2 + zl, y * 2 + oz, y_up * 2 + zl, y_down * 2 + zl, y * 2 + zl):
                self.join(q)

        def add(self, q, slots, first=0, count=ROWS):
            at = (c * 8 + q, slice(first, first + count), self.cols)
            total = ka[at].astype(F32)
            for slot in slots:
                total = total + self.rb[slot, first : first + count, self.cols].astype(F32)
            ka[at] = total.astype(BF16)

        def second(self):
            self.hops[0].wait_recv()
            self.add(y_far * 2 + zl, (0,))
            self.hops[3].start()
            self.hops[4].start()
            self.hops[1].wait_recv()
            self.hops[2].wait_recv()
            self.add(y * 2 + 1 - zl, (1, 2))
            self.hops[5].start()

        def third(self):
            self.hops[3].wait_recv()
            self.add(y_up * 2 + zl, (3,), 0, 64)
            self.hops[6].start()
            self.hops[4].wait_recv()
            self.add(y_down * 2 + zl, (3,), 64, 64)
            self.hops[7].start()

        def finish(self):
            for i in (5, 6, 7):
                self.hops[i].wait_recv()
            total = ka[c * 8 + y * 2 + zl, 0:ROWS, self.cols].astype(F32)
            for slot in (4, 5, 6):
                total = total + self.rb[slot, :, self.cols].astype(F32)
            return total.astype(BF16)

        def drain(self):
            for r in self.hops + self.twin:
                r.wait_send()

    left = Scatter(0, sb1, rb1, s1_sem, r1_sem)
    right = Scatter(1, sb1, rb1, s1_sem, r1_sem)
    left.start()
    first_pass(1, 0, 6)
    left.first()
    first_pass(1, 6, 12)
    left.second()
    def own_values(half):
        cols = slice(half * HALF, (half + 1) * HALF)
        total = vp[c * 4 + x, :, cols].astype(F32) + vsib[x, :, cols].astype(F32)
        for o in range(3):
            vx[half][o].wait_recv()
            total = total + vrow[o, :, cols].astype(F32)
        va[d, :, cols] = total.astype(BF16)

    vals = [
        Gather(va, ROWS, v_sem, vf_sem, half * 2, pl.ds(half * HALF, HALF)) for half in range(2)
    ]

    gx = [[], []]
    gf = [[], []]

    def grad_hop(half, slot, sems, i, dev):
        part = gva.at[slot, :, pl.ds(half * HALF, HALF)]
        r = remote(part, part, sems.at[half * 2, i], sems.at[half * 2 + 1, i], dev)
        r.start()
        return r

    def grads_out(half, total):
        gva[me_line, :, half * HALF : (half + 1) * HALF] = total
        for o, dx in enumerate((2, 1, 3)):
            gx[half] += [grad_hop(half, me_line, gx_sem, o, device(y, zl, c, zh, lax.rem(x + dx, 4)))]
        gf[half] += [grad_hop(half, me_line, gf_sem, 3, sib)]

    def grads_on(half):
        for o, dx in enumerate((2, 1, 3)):
            gx[half][o].wait_recv()
            gf[half] += [grad_hop(half, c * 4 + lax.rem(x - dx + 4, 4), gf_sem, o, sib)]

    def take_values(half):
        cols = slice(half * HALF, (half + 1) * HALF)
        vals[half].take(range(8), lambda q: take_pair(va, xb, q, cols))
        take_over(va, xb, cols)

    own_values(0)
    vals[0].start()
    first_pass(1, 12, 16)
    left.third()
    right.start()
    vals[0].second()
    own_values(1)
    vals[1].start()
    right.first()
    grads_out(0, left.finish())
    vals[0].third()
    right.second()
    vals[1].second()
    vals[0].fourth()
    right.third()
    vals[1].third()
    grads_out(1, right.finish())
    take_values(0)

    def second_pass(half, first, last):
        def block_step(t, _):
            heads = range(half * 4, half * 4 + 4)
            cols = [slice(g * HD, (g + 1) * HD) for g in heads]
            grad_probs = [dot_nt(xb[t, :, :, at].reshape(KEYS, HD), gos[t, g]) for g, at in zip(heads, cols)]
            lows = [probs[t, g].astype(F32) for g in heads]
            row_dots = [jnp.sum(low * v, axis=0, keepdims=True) for low, v in zip(lows, grad_probs)]
            grad_scores = [
                (low * (v - dots)).astype(BF16) for low, v, dots in zip(lows, grad_probs, row_dots)
            ]
            key_parts = [dot(v, qs[t, g]) * INV_ROOT for v, g in zip(grad_scores, heads)]
            query_parts = [
                dot_tn(v, xa[t, :, :, at].reshape(KEYS, HD)) * INV_ROOT
                for v, at in zip(grad_scores, cols)
            ]
            for g, at, key_part, query_part in zip(heads, cols, key_parts, query_parts):
                xb[t, :, :, at] = key_part.astype(BF16).reshape(10, SLOTS, HD)
                qs[t, g] = query_part.astype(BF16)
            return 0

        lax.fori_loop(first, last, block_step, 0)

    second_pass(0, 0, 8)
    vals[1].fourth()
    grads_on(0)
    second_pass(0, 8, 16)
    left.drain()
    right.drain()
    last_left = Scatter(0, sb2, rb2, s2_sem, r2_sem)
    last_right = Scatter(1, sb2, rb2, s2_sem, r2_sem)
    last_left.start()
    grads_on(1)
    take_values(1)
    last_left.first()
    for r in vx[0] + vx[1] + [v_sib]:
        r.wait_send()
    for r in gf[0] + gf[1]:
        r.wait_recv()

    def input_term(n, _):
        h, first = n // 2, pl.multiple_of(lax.rem(n, 2) * 256, 256)
        part = dot_nt(gva[...].reshape(1024, KVW), wm[h, pl.ds(first, 256), :])
        cols = pl.ds(pl.multiple_of(n * 256, 256), 256)
        vp[:, :, cols] = part.astype(BF16).reshape(8, ROWS, 256)
        return 0

    gi_copies = []
    gi_own = []
    for h in range(2):
        lax.fori_loop(h * 2, h * 2 + 2, input_term, 0)
        gi_cols = pl.ds(pl.multiple_of(h * 4096 + x * 1024 + c * HALF, HALF), HALF)
        for o, step in enumerate(LINE_STEPS):
            tx, tc = line_at(step)
            r = remote(
                vp.at[tc * 4 + tx, :, pl.ds(h * HALF, HALF)], gi_ref.at[:, gi_cols],
                gi_sem.at[0, o * 2 + h], gi_sem.at[1, o * 2 + h], line_dev(step),
            )
            r.start()
            gi_copies += [r]
        e = pltpu.make_async_copy(
            vp.at[me_line, :, pl.ds(h * HALF, HALF)], gi_ref.at[:, gi_cols], loc_sem.at[20 + h]
        )
        e.start()
        gi_own += [e]

    for h in range(2):
        for n in range(4):
            part = dot_tn(
                li[h].reshape(1024, HALF), gva[:, :, n * 256 : (n + 1) * 256].reshape(1024, 256)
            )
            part = part.astype(BF16).reshape(8, 64, 256)
            cols = slice((n % 2) * 256, (n % 2) * 256 + 256)
            for fb in range(8):
                zt, x1, x0 = fb // 4, (fb // 2) % 2, fb % 2
                if n < 2:
                    ga[zt * 2 + x0, h * 2 + x1, :, cols] = part[fb]
                else:
                    gb[h * 2 + x1, zt * 2 + x0, :, cols] = part[fb]
    g1 = []
    for i in range(3):
        r = remote(ga.at[lax.rem(z + i + 1, 4)], ra.at[i], g1_sem.at[0, i], g1_sem.at[1, i], z_devs[i])
        r.start()
        g1 += [r]
        r = remote(
            gb.at[lax.rem(y + i + 1, 4)], rbb.at[i], g1_sem.at[0, 3 + i], g1_sem.at[1, 3 + i], y_devs[i]
        )
        r.start()
        g1 += [r]

    last_left.second()
    second_pass(1, 0, 8)
    last_left.third()
    second_pass(1, 8, 16)
    last_right.start()
    for v in vals:
        v.drain()

    q_out = []

    def queries_out(g):
        slots = jnp.concatenate(
            [qs[:, g, h * SLOTS : (h + 1) * SLOTS, :].reshape(256, HD) for h in range(GROUP)], axis=1
        )
        va[g] = dot_tn(own_sel, slots).astype(BF16)
        e = pltpu.make_async_copy(va.at[g], gq_ref.at[:, pl.ds(g * 1024, 1024)], out_sem.at[g])
        e.start()
        q_out.append(e)

    for g in range(4):
        queries_out(g)
    last_right.first()
    gk_ref[:, 0:HALF] = last_left.finish()
    for r in g1:
        r.wait_recv()
    ga[z] = (
        ga[z].astype(F32) + ra[0].astype(F32) + ra[1].astype(F32) + ra[2].astype(F32)
    ).astype(BF16)
    gb[y] = (
        gb[y].astype(F32) + rbb[0].astype(F32) + rbb[1].astype(F32) + rbb[2].astype(F32)
    ).astype(BF16)

    def owners():
        for i in range(4):
            h, x1 = i // 2, i % 2
            ty, tx = 2 * h + x // 2, x1 * 2 + zl
            yield (
                in_own_line & (ty == y) & (tx == x), device(ty, lax.rem(x, 2), c, zh, tx),
                ga.at[z, i], gwa.at[y], g2s_sem.at[i], g2r_sem.at[y],
            )
            zt, x0 = i // 2, i % 2
            ty, tx = 2 * (y // 2) + x // 2, lax.rem(y, 2) * 2 + x0
            yield (
                in_own_line & (zt == zh) & (tx == x), device(ty, lax.rem(x, 2), c, zt, tx),
                gb.at[y, i], gwb.at[z], g2s_sem.at[4 + i], g2r_sem.at[4 + z],
            )

    for to_self, dev, src, dst, ssem, rsem in owners():

        @pl.when(to_self)
        def _():
            pltpu.make_async_copy(src, dst, rsem).start()

        @pl.when(jnp.logical_not(to_self))
        def _():
            remote(src, dst, ssem, rsem, dev).start()

    for g in range(4, KVH):
        queries_out(g)
    last_right.second()
    last_right.third()
    for i in range(4):
        pltpu.make_async_copy(gwa.at[i], gwa.at[i], g2r_sem.at[i]).wait()
        pltpu.make_async_copy(gwb.at[i], gwb.at[i], g2r_sem.at[4 + i]).wait()
    gw_ref[:, 0:HALF] = (gwa[0].astype(F32) + gwa[1].astype(F32)) + (gwa[2].astype(F32) + gwa[3].astype(F32))
    gw_ref[:, HALF:] = (gwb[0].astype(F32) + gwb[1].astype(F32)) + (gwb[2].astype(F32) + gwb[3].astype(F32))
    gk_ref[:, HALF:] = last_right.finish()

    for r in gi_copies:
        r.wait()
    for e in gi_own + q_out:
        e.wait()
    for r in li_copies + [w_copy] + gx[0] + gx[1] + gf[0] + gf[1] + g1:
        r.wait_send()
    last_left.drain()
    last_right.drain()
    for to_self, dev, src, dst, ssem, rsem in owners():

        @pl.when(jnp.logical_not(to_self))
        def _():
            remote(src, dst, ssem, rsem, dev).wait_send()


def shards(layer_input, queries, key_rows, grad_out, w_value, destination, seg_start):
    any_spec = pl.BlockSpec(memory_space=pl.ANY)
    vmem_spec = pl.BlockSpec(memory_space=pltpu.VMEM)
    dma = pltpu.SemaphoreType.DMA
    tokens = pltpu.VMEM
    return pl.pallas_call(
        kernel,
        out_shape=(
            jax.ShapeDtypeStruct(queries.shape, BF16),
            jax.ShapeDtypeStruct(key_rows.shape, BF16),
            jax.ShapeDtypeStruct(layer_input.shape, BF16),
            jax.ShapeDtypeStruct((64, KVW), F32),
        ),
        in_specs=[any_spec] * 5 + [vmem_spec] * 2,
        out_specs=(any_spec, vmem_spec, any_spec, vmem_spec),
        scratch_shapes=[
            tokens((RANKS, ROWS + SLOTS, KVW), BF16),
            tokens((RANKS, ROWS, KVW), BF16),
            tokens((RANKS, KVH, ROWS, HD), BF16),
            tokens((RANKS, KVH, ROWS, HD), BF16),
            tokens((RANKS, 10, SLOTS, KVW), BF16),
            tokens((RANKS, 10, SLOTS, KVW), BF16),
            tokens((RANKS, KVH, KEYS, ROWS), BF16),
            tokens((2, 8, ROWS, HALF), BF16),
            tokens((2, HALF, KVW), BF16),
            tokens((8, ROWS, KVW), BF16),
            tokens((4, ROWS, KVW), BF16),
            tokens((3, ROWS, KVW), BF16),
            tokens((8, ROWS, KVW), BF16),
            tokens((7, ROWS, KVW), BF16),
            tokens((8, ROWS, KVW), BF16),
            tokens((7, ROWS, KVW), BF16),
            tokens((8, ROWS, KVW), BF16),
            tokens((4, 4, 64, HALF), BF16),
            tokens((4, 4, 64, HALF), BF16),
            tokens((3, 4, 64, HALF), BF16),
            tokens((3, 4, 64, HALF), BF16),
            tokens((4, 64, HALF), BF16),
            tokens((4, 64, HALF), BF16),
            tokens((8, 256, 256), BF16),
            tokens((2, 256, 1024), BF16),
            tokens((RANKS, 10, SLOTS, ROWS), BF16),
            tokens((2, 256, ROWS), F32),
            tokens((RANKS, SLOTS, ROWS), F32),
            tokens((RANKS, SLOTS, ROWS), F32),
            dma((22,)),
            dma((4, 8)),
            dma((4, 8)),
            dma((4, 8)),
            dma((4, 8)),
            dma((2, 14)),
            dma((2,)),
            dma((2,)),
            dma((4, 3)),
            dma((4, 8)),
            dma((4, 8)),
            dma((4, 8)),
            dma((4, 8)),
            dma((4, 3)),
            dma((4, 4)),
            dma((2, 14)),
            dma((2, 6)),
            dma((8,)),
            dma((8,)),
            dma((8,)),
        ],
        name="packed_backward",
        compiler_params=pltpu.CompilerParams(
            collective_id=0, has_side_effects=True, vmem_limit_bytes=64 * 1024 * 1024
        ),
    )(
        layer_input, queries, key_rows, grad_out, w_value,
        destination.reshape(1, ROWS), seg_start.reshape(1, ROWS),
    )


def solution(mesh):
    both = P(("dp", "fsdp"), None)
    return jax.shard_map(
        shards,
        mesh=mesh,
        in_specs=(both, both, both, both, P("fsdp", None), P(("dp", "fsdp")), P(("dp", "fsdp"))),
        out_specs=(both, both, both, both),
        check_vma=False,
    )
```
